512 devices in a mesh: space: 16 (over y, z_lo), mem: 32 (over z_hi, x, core).
Axes of the slice: x: 4, y: 4, z: 16 (z_hi: 4, z_lo: 4; z = z_hi * 4 + z_lo), core: 2. Of those that a mesh axis runs over, the one named last changes fastest.
Arguments:
- increment: bfloat16 [1, 1024, 2304], P(None, 'space'), may hold values from -6 to 6
- mask: int32 [1, 1024, 2304], P(None, 'space'), may hold values 0 or 1
- members: bfloat16 [32, 1, 1024, 2304], P('mem', None, 'space'), may hold values from -12 to 12
- weight: float32 [1024, 2304], P('space'), may hold values from 0.5 to 2
- x_inverse: bfloat16 [18, 128, 128], replicated, may hold values from -0.0755 to 1.15
- x_coupling: float32 [17], replicated, may hold values from 0.1 to 0.5
- y_inverse: bfloat16 [8, 128, 128], replicated, may hold values from -0.0755 to 1.15
- y_coupling: float32 [7], replicated, may hold values from 0.1 to 0.5
Outputs:
- covariance_product: bfloat16 [1, 1024, 2304], P(None, 'space')
The draws below stay inside these ranges and needn't reach their ends.
All inputs are finite; a program needn't handle non-finite values. No bound on the sum of `mask` on one device may be relied on, other than what follows from the above.
Results may differ from the reference program's by a relative error of at most 0.013.
Values may be sent and summed in bfloat16 or wider, within the bound.
No kernel may reach another device: no remote copies, remote signals or barrier semaphores. Data moves between devices by JAX's collectives and lax.ppermute only.
A program may use at most 64 MiB of HBM per device.

```python
import math
import jax
import jax.numpy as jnp
from jax import lax

BLOCK = 128
NX = 2304
LEV = 1
NSTEP = 7
NY = 1024
MEMBERS = 32


def draw_x_inverse(key, part):
    key = jax.random.fold_in(key, 11)
    count = NX // BLOCK
    diag_key, other_key = jax.random.split(key)
    diagonal = jax.random.uniform(diag_key, (count, BLOCK), jnp.float32, 0.85, 1.15)
    others = jnp.clip(jax.random.normal(other_key, (count, BLOCK, BLOCK), jnp.float32), -5.0, 5.0) * 0.015
    identity = jnp.eye(BLOCK, dtype=jnp.float32)[None]
    return (others * (1.0 - identity) + identity * diagonal[:, :, None]).astype(jnp.bfloat16)


def draw_y_inverse(key, part):
    key = jax.random.fold_in(key, 23)
    count = NY // BLOCK
    diag_key, other_key = jax.random.split(key)
    diagonal = jax.random.uniform(diag_key, (count, BLOCK), jnp.float32, 0.85, 1.15)
    others = jnp.clip(jax.random.normal(other_key, (count, BLOCK, BLOCK), jnp.float32), -5.0, 5.0) * 0.015
    identity = jnp.eye(BLOCK, dtype=jnp.float32)[None]
    return (others * (1.0 - identity) + identity * diagonal[:, :, None]).astype(jnp.bfloat16)


def with_ends(values, own_key, smallest, top_value):
    extent = values.shape
    index_at = [jax.random.randint(jax.random.fold_in(own_key, axis), (), 0, extent[axis]) for axis in range(len(extent))]
    values = values.at[tuple(index_at)].set(smallest)
    longest = extent.index(max(extent))
    index_at[longest] = (index_at[longest] + 1) % extent[longest]
    return values.at[tuple(index_at)].set(top_value)


def steps_of(stream_key, shape, shards, low, high):
    loudness, own = 1.0, jax.random.fold_in(stream_key, 6)
    for axis_at, blocks in shards:
        heights = jnp.exp(jax.random.uniform(jax.random.fold_in(own, axis_at), (blocks,), jnp.float32, low / len(shards), high / len(shards)))
        loudness = loudness * jnp.repeat(heights, shape[axis_at] // blocks).reshape([-1 if axis == axis_at else 1 for axis in range(len(shape))])
    return loudness


def centred(rng, dims, width, limit, shards=(), held_as=jnp.bfloat16):
    level = steps_of(rng, dims, shards, -0.22, 0.18) if shards else 1.0
    values = jax.random.normal(rng, dims, jnp.float32) * width * level
    return jnp.minimum(jnp.maximum(values, -limit), limit).astype(held_as)


def setup_inputs(seed: int = 0) -> dict:
    splits = jax.random.split(jax.random.key(seed), 9)
    increment = centred(splits[0], (LEV, NY, NX), 1.0, 6.0, ((1, 16),))
    mask = with_ends((jax.random.randint(splits[1], (LEV, NY, NX), 0, 4) < 3).astype(jnp.int32), jax.random.fold_in(splits[1], 1), 0, 1)
    members = centred(splits[2], (MEMBERS, LEV, NY, NX), 2.0, 12.0, ((0, 32), (2, 16)))
    weight = jnp.clip(jnp.exp(math.log(2.0) - 1.3862944 * jax.random.uniform(splits[3], (NY, NX), jnp.float32) ** steps_of(splits[3], (NY, NX), ((0, 16),), -0.2, 0.2)), 0.5, 2.0)
    x_inverse = draw_x_inverse(jax.random.fold_in(splits[8], 71), 0)
    x_coupling = jnp.clip(jnp.exp(jax.random.uniform(splits[5], (NX // BLOCK - 1,), jnp.float32, math.log(0.1), math.log(0.5))), 0.1, 0.5)
    y_inverse = draw_y_inverse(jax.random.fold_in(splits[8], 71), 0)
    y_coupling = jnp.clip(jnp.exp(jax.random.uniform(splits[7], (NY // BLOCK - 1,), jnp.float32, math.log(0.1), math.log(0.5))), 0.1, 0.5)
    return dict(increment=increment, mask=mask, members=members, weight=weight, x_inverse=x_inverse, x_coupling=x_coupling, y_inverse=y_inverse, y_coupling=y_coupling)


def products(blocked, inverse, adjoint, lines_last):
    if lines_last:
        pattern = "ankl,nkj->anjl" if adjoint else "ankl,njk->anjl"
    else:
        pattern = "alnk,nkj->alnj" if adjoint else "alnk,njk->alnj"
    return jnp.einsum(pattern, blocked.astype(jnp.float32), inverse.astype(jnp.float32), precision=lax.Precision.HIGHEST)


def entries(product, position, lines_last):
    if lines_last:
        return jnp.moveaxis(product[:, :, position, :], 1, 0)
    return jnp.moveaxis(product[:, :, :, position], 2, 0)


def spread(scalars, column, lines_last):
    if lines_last:
        return jnp.moveaxis(scalars, 0, 1)[:, :, None, :] * column[None, :, :, None]
    return jnp.moveaxis(scalars, 0, 2)[:, :, :, None] * column[None, None, :, :]


def recur_step(carried, inputs):
    source, factor, coupler = inputs
    updated = coupler * (source + factor * carried)
    return updated, updated


def run_upward(sources, factor, coupling):
    anchor = jnp.zeros_like(sources[0])
    _, following = lax.scan(recur_step, anchor, (sources[:-1], factor[:-1], coupling))
    return jnp.concatenate([jnp.zeros_like(sources[:1]), following], 0)


def run_downward(sources, factor, coupling):
    anchor = jnp.zeros_like(sources[0])
    _, earlier = lax.scan(recur_step, anchor, (sources[1:], factor[1:], coupling), reverse=True)
    return jnp.concatenate([earlier, jnp.zeros_like(sources[:1])], 0)


def forward_solve(blocked, inverse, coupling, lines_last):
    ending = inverse.shape[1] - 1
    inv_float = inverse.astype(jnp.float32)
    product = products(blocked, inverse, False, lines_last)
    leading = run_upward(entries(product, ending, lines_last), inv_float[:, ending, 0], coupling)
    first_row = entries(product, 0, lines_last) + leading * inv_float[:, 0, 0][:, None, None]
    trailing = run_downward(first_row, inv_float[:, 0, ending], coupling)
    result = product + spread(leading, inv_float[:, :, 0], lines_last) + spread(trailing, inv_float[:, :, ending], lines_last)
    return result.astype(jnp.bfloat16)


def adjoint_solve(blocked, inverse, coupling, lines_last):
    ending = inverse.shape[1] - 1
    inv_float = inverse.astype(jnp.float32)
    product = products(blocked, inverse, True, lines_last)
    leading = run_upward(entries(product, ending, lines_last), inv_float[:, 0, ending], coupling)
    first_row = entries(product, 0, lines_last) + leading * inv_float[:, 0, 0][:, None, None]
    trailing = run_downward(first_row, inv_float[:, ending, 0], coupling)
    result = product + spread(leading, inv_float[:, 0, :], lines_last) + spread(trailing, inv_float[:, ending, :], lines_last)
    return result.astype(jnp.bfloat16)


def reference(increment, mask, members, weight, x_inverse, x_coupling, y_inverse, y_coupling):
    levels, lat_rows, lon_cols = increment.shape
    land_sea = mask.astype(jnp.float32)

    def one_member(summed, member):
        member_float = member.astype(jnp.float32)
        values = (weight[None] * land_sea * member_float * increment.astype(jnp.float32)).astype(jnp.bfloat16)
        blocked = values.reshape(levels, lat_rows, lon_cols // BLOCK, BLOCK)
        for repeat in range(NSTEP):
            blocked = adjoint_solve(blocked, x_inverse, x_coupling, False)
        blocked = blocked.reshape(levels, lat_rows // BLOCK, BLOCK, lon_cols)
        for repeat in range(NSTEP):
            blocked = adjoint_solve(blocked, y_inverse, y_coupling, True)
        for repeat in range(NSTEP):
            blocked = forward_solve(blocked, y_inverse, y_coupling, True)
        blocked = blocked.reshape(levels, lat_rows, lon_cols // BLOCK, BLOCK)
        for repeat in range(NSTEP):
            blocked = forward_solve(blocked, x_inverse, x_coupling, False)
        smoothed = blocked.reshape(levels, lat_rows, lon_cols).astype(jnp.float32)
        return summed + member_float * weight[None] * smoothed, None

    summed, _ = lax.scan(one_member, jnp.zeros((levels, lat_rows, lon_cols), jnp.float32), members)
    return (land_sea * summed / (MEMBERS - 1)).astype(jnp.bfloat16)
```

```python
import functools

import jax
import jax.numpy as jnp
from jax import lax
from jax.experimental import pallas as pl
from jax.experimental.pallas import tpu as pltpu
from jax.sharding import PartitionSpec as P


BLOCK = 128
LAST = BLOCK - 1
NSTEP = 7
HALF = 64
EXTRA = 16
F32 = jnp.float32
BF16 = jnp.bfloat16
VMEM_LIMIT = 50 * 2**20


def dot(a, b):
    return lax.dot_general(a, b, (((1,), (0,)), ((), ())), preferred_element_type=F32)


def dot_nt(a, b):
    return lax.dot_general(a, b, (((1,), (1,)), ((), ())), preferred_element_type=F32)


def round_up(value, unit):
    return (value + unit - 1) // unit * unit


def coupling_rows(nb, depth):
    return round_up(2 * NSTEP * nb, depth)


def prepare_kernel(nb, group, c_ref, g_ref, pow_ref, kta_ref, ktf_ref, rb_ref, cb_ref,
                   rs, cs, big, rmat, qmat, ct):
    pad = round_up(nb, 8)
    kp = ct.shape[0]
    width = nb * BLOCK
    select = jnp.where(
        lax.broadcasted_iota(jnp.int32, (16, BLOCK), 1)
        == lax.broadcasted_iota(jnp.int32, (16, BLOCK), 0) * LAST, 1.0, 0.0).astype(BF16)
    rs[...] = jnp.zeros_like(rs)
    cs[...] = jnp.zeros_like(cs)

    def one(j):
        g = g_ref[j]
        powers = {1: (g, g.astype(F32))}

        def mul(k, a, b):
            full = dot(powers[a][0], powers[b][0])
            powers[k] = (full.astype(BF16), full)

        mul(2, 1, 1)
        mul(3, 2, 1)
        mul(4, 2, 2)
        mul(5, 3, 2)
        mul(6, 4, 2)
        mul(7, 4, 3)
        pow_ref[j] = powers[NSTEP][0]
        for k in range(1, NSTEP + 1):
            low, full = powers[k]
            rs[k - 1, 0, pl.ds(j, 1), :] = full[0:1, :]
            rs[k - 1, 1, pl.ds(j, 1), :] = full[LAST:BLOCK, :]
            columns = dot_nt(select, low)
            cs[k - 1, 0, pl.ds(j, 1), :] = columns[0:1, :]
            cs[k - 1, 1, pl.ds(j, 1), :] = columns[1:2, :]

    def some(i, carry):
        for offset in range(group):
            one(i * group + offset)
        return carry

    lax.fori_loop(0, nb // group, some, 0)

    own = (lax.broadcasted_iota(jnp.int32, (nb, width), 1) // BLOCK
           == lax.broadcasted_iota(jnp.int32, (nb, width), 0))
    for source, target in ((rs, rb_ref), (cs, cb_ref)):
        big[...] = jnp.zeros_like(big)
        for k in range(1, NSTEP + 1):
            for kind in range(2):
                stacked = source[k - 1, 1 - kind, 0:nb, :]
                wide = jnp.concatenate([stacked] * nb, axis=1)
                at = ((k - 1) * 2 + kind) * nb
                big[at:at + nb, :] = jnp.where(own, wide, 0.0)
        target[...] = big[...].astype(BF16)

    lane = lax.broadcasted_iota(jnp.int32, (1, BLOCK), 1)
    row = lax.broadcasted_iota(jnp.int32, (pad, kp), 0)
    lanes = lax.broadcasted_iota(jnp.int32, (pad, kp), 1)
    for adjoint, kt_ref, edge_ref in ((True, kta_ref, cb_ref), (False, ktf_ref, rb_ref)):
        def corner(k, a, b):
            if not adjoint:
                a, b = b, a
            return rs[k - 1, a, :, 0:1] if b == 0 else rs[k - 1, a, :, LAST:BLOCK]

        gain_s = jnp.broadcast_to(corner(1, 0, 1), (pad, BLOCK))
        gain_t = jnp.broadcast_to(corner(1, 1, 0), (pad, BLOCK))
        gain_0 = jnp.broadcast_to(corner(1, 0, 0), (pad, BLOCK))
        rmat[...] = jnp.zeros_like(rmat)
        s_row = jnp.zeros((1, BLOCK), F32)
        p_rows = []
        for j in range(nb):
            p_rows.append(jnp.where(lane == pad + j, 1.0, 0.0) + gain_0[j:j + 1] * s_row)
            if j + 1 < nb:
                s_row = c_ref[j] * (jnp.where(lane == j, 1.0, 0.0) + gain_s[j:j + 1] * s_row)
                rmat[j + 1:j + 2, :] = s_row
        t_row = jnp.zeros((1, BLOCK), F32)
        for j in range(nb - 2, -1, -1):
            t_row = c_ref[j] * (p_rows[j + 1] + gain_t[j + 1:j + 2] * t_row)
            rmat[pad + j:pad + j + 1, :] = t_row
        spread = rmat[...]

        qmat[...] = jnp.zeros_like(qmat)
        ct[...] = jnp.zeros_like(ct)
        sources, trailing = [], []
        for k in range(NSTEP):
            at = 2 * k * nb
            real = row < nb
            q_last = jnp.where(real & (lanes == at + row), 1.0, 0.0)
            q_first = jnp.where(real & (lanes == at + nb + row), 1.0, 0.0)
            for m in range(k):
                q_last += corner(k - m + 1, 0, 1) * sources[m] + corner(k - m + 1, 1, 1) * trailing[m]
                q_first += corner(k - m + 1, 0, 0) * sources[m] + corner(k - m + 1, 1, 0) * trailing[m]
            qmat[0:pad, :] = q_last
            qmat[pad:2 * pad, :] = q_first
            both = lax.dot_general(spread, qmat[...], (((1,), (0,)), ((), ())),
                                   precision=lax.Precision.HIGHEST, preferred_element_type=F32)
            s_now, t_now = both[0:pad], both[pad:2 * pad]
            sources.append(s_now)
            trailing.append(t_now)
            place = (NSTEP - 1 - k) * 2 * nb
            ct[place:place + nb, :] = t_now[0:nb]
            ct[place + nb:place + 2 * nb, :] = s_now[0:nb]
        kt_ref[...] = dot(ct[...].astype(BF16), edge_ref[...]).astype(BF16)


def prepare(inverse, coupling, group):
    nb = inverse.shape[0]
    width = nb * BLOCK
    kp = coupling_rows(nb, BLOCK)
    pad = round_up(nb, 8)
    vmem = pl.BlockSpec(memory_space=pltpu.VMEM)
    table = jax.ShapeDtypeStruct((kp, width), BF16)
    return pl.pallas_call(
        functools.partial(prepare_kernel, nb, group),
        out_shape=(jax.ShapeDtypeStruct((nb, BLOCK, BLOCK), BF16), table, table, table, table),
        in_specs=[pl.BlockSpec(memory_space=pltpu.SMEM), vmem],
        out_specs=(vmem,) * 5,
        scratch_shapes=[
            pltpu.VMEM((NSTEP, 2, pad, BLOCK), F32),
            pltpu.VMEM((NSTEP, 2, pad, BLOCK), F32),
            pltpu.VMEM((kp, width), F32),
            pltpu.VMEM((2 * pad, BLOCK), F32),
            pltpu.VMEM((BLOCK, kp), F32),
            pltpu.VMEM((kp, kp), F32),
        ],
        compiler_params=pltpu.CompilerParams(vmem_limit_bytes=VMEM_LIMIT),
        cost_estimate=pl.CostEstimate(
            flops=nb * 20 * 2 * BLOCK**3, bytes_accessed=10 * kp * width, transcendentals=0),
    )(coupling, inverse)


def run_steps(lines, nb, pow_ref, kt_ref, out_ref, adjoint):
    coupled = dot_nt(lines[...], kt_ref[...]).astype(BF16)
    results = []
    for j in range(nb):
        at = slice(j * BLOCK, (j + 1) * BLOCK)
        own = (dot if adjoint else dot_nt)(lines[:, at], pow_ref[j])
        results.append(own + dot(coupled, out_ref[:, at]))
    return results


def start_kernel(increment_ref, mask_ref, members_ref, weight_ref, out_ref):
    values = (weight_ref[...] * mask_ref[0].astype(F32) * members_ref[0, 0].astype(F32)
              * increment_ref[0].astype(F32))
    shares = out_ref.shape[0]
    for s in range(shares):
        out_ref[s, 0:HALF, :] = values[:, s * BLOCK:(s + 1) * BLOCK].astype(BF16)
    for half in range(2):
        at = (shares + half) * BLOCK
        tail = values[:, at:at + BLOCK]
        turned = jnp.concatenate([tail, tail], axis=0).T
        for s in range(8):
            out_ref[half * 8 + s, HALF:HALF + EXTRA, :] = turned[s * EXTRA:(s + 1) * EXTRA].astype(BF16)


def column_kernel(nb, in_ref, pow_ref, kta_ref, ktf_ref, rb_ref, cb_ref, out_ref, lines):
    for j in range(nb):
        at = slice(j * BLOCK, (j + 1) * BLOCK)
        square = jnp.concatenate([in_ref[2 * j, 0:HALF, :], in_ref[2 * j + 1, 0:HALF, :]], axis=0)
        lines[0:BLOCK, at] = square.astype(F32).T.astype(BF16)
        lane = lax.broadcasted_iota(jnp.int32, (EXTRA, BLOCK), 1)
        tail = jnp.where(lane < HALF, in_ref[2 * j, HALF:HALF + EXTRA, :].astype(F32),
                         in_ref[2 * j + 1, HALF:HALF + EXTRA, :].astype(F32))
        lines[BLOCK:BLOCK + EXTRA, at] = tail.astype(BF16)
    for j, block in enumerate(run_steps(lines, nb, pow_ref, kta_ref, rb_ref, True)):
        lines[:, j * BLOCK:(j + 1) * BLOCK] = block.astype(BF16)
    for j, block in enumerate(run_steps(lines, nb, pow_ref, ktf_ref, cb_ref, False)):
        square = block[0:BLOCK].T.astype(BF16)
        tail = block[BLOCK:BLOCK + EXTRA].astype(BF16)
        for half in range(2):
            out_ref[2 * j + half, 0:HALF, :] = square[half * HALF:(half + 1) * HALF]
            out_ref[2 * j + half, HALF:HALF + EXTRA, :] = tail


def row_kernel(nb, parity_ref, in_ref, members_ref, weight_ref, pow_ref, kta_ref, ktf_ref, rb_ref, cb_ref,
               out_ref, lines):
    shares = in_ref.shape[0]
    for s in range(shares):
        lines[:, s * BLOCK:(s + 1) * BLOCK] = in_ref[s, 0:HALF, :]
    odd = parity_ref[0] == 1
    for half in range(2):
        tail = jnp.concatenate(
            [in_ref[half * 8 + s, HALF:HALF + EXTRA, :] for s in range(8)], axis=0).astype(F32).T
        tail = jnp.where(odd, tail[HALF:BLOCK], tail[0:HALF])
        at = (shares + half) * BLOCK
        lines[:, at:at + BLOCK] = tail.astype(BF16)
    for j, block in enumerate(run_steps(lines, nb, pow_ref, kta_ref, rb_ref, True)):
        lines[:, j * BLOCK:(j + 1) * BLOCK] = block.astype(BF16)
    takers, middle = out_ref.shape[0], nb // 2
    blocks = run_steps(lines, nb, pow_ref, ktf_ref, cb_ref, False)
    for j in range(middle):
        left, right = slice(j * BLOCK, (j + 1) * BLOCK), slice((middle + j) * BLOCK, (middle + j + 1) * BLOCK)
        term_left = members_ref[0, 0, :, left].astype(F32) * weight_ref[:, left] * blocks[j]
        term_right = members_ref[0, 0, :, right].astype(F32) * weight_ref[:, right] * blocks[middle + j]
        for taker in range(takers):
            rows = slice(taker * 8, taker * 8 + 8)
            out_ref[taker, :, left] = jnp.concatenate([term_left[rows], term_right[rows]], axis=0).astype(BF16)


def sum_kernel(scale, in_ref, out_ref):
    total = in_ref[0].astype(F32)
    for source in range(1, in_ref.shape[0]):
        total += in_ref[source].astype(F32)
    if scale is not None:
        total = total / scale
    total = total.astype(BF16)
    for target in range(out_ref.shape[0]):
        out_ref[target] = total


def final_kernel(mask_ref, in_ref, out_ref):
    shares, _, width = in_ref.shape
    for pair in range(shares // 2):
        one, two = in_ref[2 * pair].astype(F32), in_ref[2 * pair + 1].astype(F32)
        rows = slice(pair * 16, pair * 16 + 16)
        left = jnp.concatenate([one[0:8], two[0:8]], axis=0)
        right = jnp.concatenate([one[8:16], two[8:16]], axis=0)
        out_ref[0, rows, 0:width] = (left * mask_ref[0, rows, 0:width].astype(F32)).astype(BF16)
        out_ref[0, rows, width:2 * width] = (right * mask_ref[0, rows, width:2 * width].astype(F32)).astype(BF16)


def call(kernel, out_shape, operands, scratch=(), scalars=0, flops=1000000):
    vmem = pl.BlockSpec(memory_space=pltpu.VMEM)
    smem = pl.BlockSpec(memory_space=pltpu.SMEM)
    return pl.pallas_call(
        kernel,
        out_shape=jax.ShapeDtypeStruct(out_shape, BF16),
        in_specs=[smem] * scalars + [vmem] * (len(operands) - scalars),
        out_specs=vmem,
        scratch_shapes=list(scratch),
        compiler_params=pltpu.CompilerParams(vmem_limit_bytes=VMEM_LIMIT),
        cost_estimate=pl.CostEstimate(flops=flops, bytes_accessed=2000000, transcendentals=0),
    )(*operands)


def exchange(array, axis, groups=None):
    return lax.all_to_all(array, axis, split_axis=0, concat_axis=0, tiled=True, axis_index_groups=groups)


def local(increment, mask, members, weight, x_inverse, x_coupling, y_inverse, y_coupling):
    _, _, rows, columns = members.shape
    space, mem = lax.axis_size("space"), lax.axis_size("mem")
    x_blocks, y_blocks = x_inverse.shape[0], y_inverse.shape[0]
    near = 8
    far = mem // near
    near_groups = [[z * near + i for i in range(near)] for z in range(far)]
    far_groups = [[z * near + i for z in range(far)] for i in range(near)]
    share = (HALF + EXTRA, BLOCK)

    y_tables = prepare(y_inverse, y_coupling, 8)
    x_tables = prepare(x_inverse, x_coupling, 6)

    sent = call(start_kernel, (space,) + share, (increment, mask, members, weight))
    got = exchange(sent, "space")
    sent = call(functools.partial(column_kernel, y_blocks), (space,) + share, (got,) + tuple(y_tables),
                [pltpu.VMEM((BLOCK + EXTRA, y_blocks * BLOCK), BF16)])
    got = exchange(sent, "space")
    parity = (lax.axis_index("space") % 2).astype(jnp.int32)[None]
    packed = (16, columns // 2)
    terms = call(functools.partial(row_kernel, x_blocks), (near,) + packed,
                 (parity, got, members, weight) + tuple(x_tables),
                 [pltpu.VMEM((rows, columns), BF16)], scalars=1)
    terms = exchange(terms, "mem", near_groups)
    terms = call(functools.partial(sum_kernel, None), (far,) + packed, (terms,))
    terms = exchange(terms, "mem", far_groups)
    terms = call(functools.partial(sum_kernel, float(mem - 1)), (near,) + packed, (terms,))
    terms = exchange(terms, "mem", near_groups)
    return call(final_kernel, (1, rows, columns), (mask, terms))


def solution(mesh):
    placed = (
        P(None, "space", None),
        P(None, "space", None),
        P("mem", None, "space", None),
        P("space", None),
        P(),
        P(),
        P(),
        P(),
    )
    return jax.shard_map(
        local, mesh=mesh, in_specs=placed, out_specs=P(None, "space", None), check_vma=False
    )
```

```python
import functools

import jax
import jax.numpy as jnp
from jax import lax
from jax.experimental import pallas as pl
from jax.experimental.pallas import tpu as pltpu
from jax.sharding import PartitionSpec as P


BLOCK = 128
LAST = BLOCK - 1
NSTEP = 7
HALF = 64
EXTRA = 16
F32 = jnp.float32
BF16 = jnp.bfloat16
VMEM_LIMIT = 24 * 2**20
WIDE_LIMIT = 60 * 2**20


def dot(a, b):
    return lax.dot_general(a, b, (((1,), (0,)), ((), ())), preferred_element_type=F32)


def dot_nt(a, b):
    return lax.dot_general(a, b, (((1,), (1,)), ((), ())), preferred_element_type=F32)


def round_up(value, unit):
    return (value + unit - 1) // unit * unit


def coupling_rows(nb, depth):
    return round_up(2 * NSTEP * nb, depth)


def prepare_kernel(nb, precise, c_ref, g_ref, *refs):
    fill_tables(nb, precise, c_ref, g_ref, *refs, lambda at: None)


def prepare_far_kernel(nb, precise, c_ref, g_ref, *refs):
    far, near, (left, *scratch) = refs[:5], refs[5:10], refs[10:]
    copies = [pltpu.make_async_copy(near[at], far[at], left.at[at]) for at in range(5)]
    fill_tables(nb, precise, c_ref, g_ref, *near, *scratch, lambda at: copies[at].start())
    for copy in copies:
        copy.wait()


def fill_tables(nb, precise, c_ref, g_ref, pow_ref, kta_ref, ktf_ref, rb_ref, cb_ref,
                   edges, big_rows, big_columns, rmat, qmat, ct,
                   high2, low2, high3, low3, high4, low4, few_rows, few_columns, ready):
    pad = round_up(nb, 8)
    kp = kta_ref.shape[0]
    lane = lax.broadcasted_iota(jnp.int32, (16, BLOCK), 1)
    row = lax.broadcasted_iota(jnp.int32, (16, BLOCK), 0)
    select = jnp.where((row < 2) & (lane == row * LAST), 1.0, 0.0)
    edges[...] = jnp.zeros_like(edges)
    big_rows[...] = jnp.zeros_like(big_rows)
    big_columns[...] = jnp.zeros_like(big_columns)

    def stack(first, *pairs):
        out = first
        for at, (top, bottom) in enumerate(pairs):
            out = jnp.where(row == 2 * at + 2, top, jnp.where(row == 2 * at + 3, bottom, out))
        return out.astype(BF16)

    def split(full):
        high = full.astype(BF16)
        return high, (full - high.astype(F32)).astype(BF16)

    def put_row(j, k, top, bottom):
        at = slice(j * BLOCK, (j + 1) * BLOCK)
        big_rows[(2 * k - 2) * nb + j:(2 * k - 2) * nb + j + 1, at] = bottom
        big_rows[(2 * k - 1) * nb + j:(2 * k - 1) * nb + j + 1, at] = top
        edges[k - 1, 0, j:j + 1, :] = top
        edges[k - 1, 1, j:j + 1, :] = bottom

    def put_column(j, k, left, right):
        at = slice(j * BLOCK, (j + 1) * BLOCK)
        big_columns[(2 * k - 2) * nb + j:(2 * k - 2) * nb + j + 1, at] = right
        big_columns[(2 * k - 1) * nb + j:(2 * k - 1) * nb + j + 1, at] = left

    def ends(full):
        return full[0:1], full[LAST:BLOCK]

    def pair(rows, first):
        return rows[first:first + 1], rows[first + 1:first + 2]

    for j in range(nb):
        g = g_ref[j]
        g_full = g.astype(F32)
        second = dot(g, g)
        high2[j], low2[j] = split(second)
        put_row(j, 1, *ends(g_full))
        put_row(j, 2, *ends(second))
        few_rows[j] = stack(jnp.zeros((16, BLOCK), F32), ends(g_full), ends(second))
        columns = dot_nt(select.astype(BF16), g)
        put_column(j, 1, *pair(columns, 0))
        few_columns[j] = stack(select, pair(columns, 0)).astype(F32)

    for j in range(nb):
        both = jnp.concatenate([g_ref[j], high2[j]], axis=0)
        if precise:
            result = dot(jnp.concatenate([both, both], axis=1),
                         jnp.concatenate([high2[j], low2[j]], axis=0))
            third, fourth = result[0:BLOCK], result[BLOCK:2 * BLOCK] + dot(low2[j], high2[j])
        else:
            result = dot(both, high2[j])
            third, fourth = result[0:BLOCK], result[BLOCK:2 * BLOCK]
        high3[j], low3[j] = split(third)
        high4[j], low4[j] = split(fourth)
        put_row(j, 3, *ends(third))
        put_row(j, 4, *ends(fourth))
        old = few_columns[j]
        columns = dot_nt(old.astype(BF16), high2[j])
        put_column(j, 2, *pair(columns, 0))
        put_column(j, 3, *pair(columns, 2))
        few_columns[j] = stack(old, pair(old, 2), pair(columns, 0), pair(columns, 2)).astype(F32)

    for j in range(nb):
        left = jnp.concatenate([high3[j], few_rows[j]], axis=0)
        if precise:
            result = dot(jnp.concatenate([left, left], axis=1),
                         jnp.concatenate([high4[j], low4[j]], axis=0))
            seventh = result[0:BLOCK] + dot(low3[j], high4[j])
        else:
            result = dot(left, high4[j])
            seventh = result[0:BLOCK]
        pow_ref[j] = seventh.astype(BF16)
        put_row(j, 5, *pair(result, BLOCK + 2))
        put_row(j, 6, *pair(result, BLOCK + 4))
        put_row(j, 7, *ends(seventh))
        columns = dot_nt(few_columns[j].astype(BF16), high4[j])
        for k in range(4):
            put_column(j, 4 + k, *pair(columns, 2 * k))

    ready(0)
    rb_ref[...] = big_rows[...].astype(BF16)
    ready(3)
    cb_ref[...] = big_columns[...].astype(BF16)
    ready(4)

    def corner(run, k, a, b):
        if run == 1:
            a, b = b, a
        return edges[k - 1, a, :, 0:1] if b == 0 else edges[k - 1, a, :, LAST:BLOCK]

    unit = lax.broadcasted_iota(jnp.int32, (1, BLOCK), 1)
    runs = range(2)
    gain_s = [jnp.broadcast_to(corner(run, 1, 0, 1), (pad, BLOCK)) for run in runs]
    gain_t = [jnp.broadcast_to(corner(run, 1, 1, 0), (pad, BLOCK)) for run in runs]
    gain_0 = jnp.broadcast_to(corner(0, 1, 0, 0), (pad, BLOCK))
    rmat[...] = jnp.zeros_like(rmat)
    qmat[...] = jnp.zeros_like(qmat)
    ct[...] = jnp.zeros_like(ct)
    s_row = [jnp.zeros((1, BLOCK), F32) for run in runs]
    p_rows = [[], []]
    for j in range(nb):
        for run in runs:
            p_rows[run].append(jnp.where(unit == pad + j, 1.0, 0.0) + gain_0[j:j + 1] * s_row[run])
            if j + 1 < nb:
                s_row[run] = c_ref[j] * (jnp.where(unit == j, 1.0, 0.0) + gain_s[run][j:j + 1] * s_row[run])
                rmat[run, j + 1:j + 2, :] = s_row[run]
    t_row = [jnp.zeros((1, BLOCK), F32) for run in runs]
    for j in range(nb - 2, -1, -1):
        for run in runs:
            t_row[run] = c_ref[j] * (p_rows[run][j + 1] + gain_t[run][j + 1:j + 2] * t_row[run])
            rmat[run, pad + j:pad + j + 1, :] = t_row[run]

    block = lax.broadcasted_iota(jnp.int32, (pad, kp), 0)
    lanes = lax.broadcasted_iota(jnp.int32, (pad, kp), 1)
    sources, trailing = [[], []], [[], []]
    for k in range(NSTEP):
        at = 2 * k * nb
        place = (NSTEP - 1 - k) * 2 * nb
        for run in runs:
            q_last = jnp.where((block < nb) & (lanes == at + block), 1.0, 0.0)
            q_first = jnp.where((block < nb) & (lanes == at + nb + block), 1.0, 0.0)
            for m in range(k):
                s_old, t_old = sources[run][m], trailing[run][m]
                q_last += corner(run, k - m + 1, 0, 1) * s_old + corner(run, k - m + 1, 1, 1) * t_old
                q_first += corner(run, k - m + 1, 0, 0) * s_old + corner(run, k - m + 1, 1, 0) * t_old
            qmat[run, 0:pad, :] = q_last
            qmat[run, pad:2 * pad, :] = q_first
        for run in runs:
            now = lax.dot_general(rmat[run], qmat[run], (((1,), (0,)), ((), ())),
                                  precision=lax.Precision.HIGHEST, preferred_element_type=F32)
            sources[run].append(now[0:pad])
            trailing[run].append(now[pad:2 * pad])
            ct[run, place:place + nb, :] = now[pad:pad + nb]
            ct[run, place + nb:place + 2 * nb, :] = now[0:nb]
    kta_ref[...] = dot(ct[0].astype(BF16), cb_ref[...]).astype(BF16)
    ready(1)
    ktf_ref[...] = dot(ct[1].astype(BF16), rb_ref[...]).astype(BF16)
    ready(2)


def prepare(inverse, coupling, precise, far):
    nb = inverse.shape[0]
    width = nb * BLOCK
    kp = coupling_rows(nb, BLOCK)
    pad = round_up(nb, 8)
    vmem = pl.BlockSpec(memory_space=pltpu.VMEM)
    table = jax.ShapeDtypeStruct((kp, width), BF16)
    tables = (jax.ShapeDtypeStruct((nb, BLOCK, BLOCK), BF16), table, table, table, table)
    staging = [pltpu.VMEM(array.shape, array.dtype) for array in tables] + [pltpu.SemaphoreType.DMA((5,))]
    return pl.pallas_call(
        functools.partial(prepare_far_kernel if far else prepare_kernel, nb, precise),
        out_shape=tables,
        in_specs=[pl.BlockSpec(memory_space=pltpu.SMEM), vmem],
        out_specs=(pl.BlockSpec(memory_space=pltpu.HBM) if far else vmem,) * 5,
        scratch_shapes=(staging if far else []) + [
            pltpu.VMEM((NSTEP, 2, pad, BLOCK), F32),
            pltpu.VMEM((kp, width), F32),
            pltpu.VMEM((kp, width), F32),
            pltpu.VMEM((2, 2 * pad, BLOCK), F32),
            pltpu.VMEM((2, BLOCK, kp), F32),
            pltpu.VMEM((2, kp, kp), F32),
        ] + [pltpu.VMEM((nb, BLOCK, BLOCK), BF16)] * 6 + [
            pltpu.VMEM((nb, 16, BLOCK), BF16),
            pltpu.VMEM((nb, 16, BLOCK), F32),
        ],
        compiler_params=pltpu.CompilerParams(vmem_limit_bytes=WIDE_LIMIT if far else VMEM_LIMIT),
        cost_estimate=pl.CostEstimate(
            flops=nb * 20 * 2 * BLOCK**3, bytes_accessed=10 * kp * width, transcendentals=0),
    )(coupling, inverse)


def run_steps(lines, nb, pow_ref, kt_ref, out_ref, adjoint, arrive=lambda *refs: None):
    arrive(kt_ref)
    coupled = dot_nt(lines[...], kt_ref[...]).astype(BF16)
    arrive(pow_ref, out_ref)
    results = []
    for j in range(nb):
        at = slice(j * BLOCK, (j + 1) * BLOCK)
        own = (dot if adjoint else dot_nt)(lines[:, at], pow_ref[j])
        results.append(own + dot(coupled, out_ref[:, at]))
    return results


def start_kernel(increment_hbm, mask_hbm, members_hbm, weight_hbm, out_ref,
                 increment_ref, mask_ref, members_ref, weight_ref, arrived):
    copies = [
        pltpu.make_async_copy(source, target, arrived.at[at])
        for at, (source, target) in enumerate((
            (increment_hbm, increment_ref), (mask_hbm, mask_ref),
            (members_hbm, members_ref), (weight_hbm, weight_ref)))
    ]
    for copy in copies:
        copy.start()
    for copy in copies:
        copy.wait()
    shares = out_ref.shape[0]

    def values(at):
        return (weight_ref[:, at] * mask_ref[0, :, at].astype(F32) * members_ref[0, 0, :, at].astype(F32)
                * increment_ref[0, :, at].astype(F32))

    for half in range(2):
        tail = values(slice((shares + half) * BLOCK, (shares + half + 1) * BLOCK))
        turned = jnp.concatenate([tail, tail], axis=0).T
        for s in range(8):
            out_ref[half * 8 + s, HALF:HALF + EXTRA, :] = turned[s * EXTRA:(s + 1) * EXTRA].astype(BF16)
    for s in range(shares):
        out_ref[s, 0:HALF, :] = values(slice(s * BLOCK, (s + 1) * BLOCK)).astype(BF16)


def column_kernel(nb, in_ref, pow_ref, kta_ref, ktf_ref, rb_ref, cb_ref, out_ref, lines):
    for j in range(nb):
        at = slice(j * BLOCK, (j + 1) * BLOCK)
        square = jnp.concatenate([in_ref[2 * j, 0:HALF, :], in_ref[2 * j + 1, 0:HALF, :]], axis=0)
        lines[0:BLOCK, at] = square.astype(F32).T.astype(BF16)
        lane = lax.broadcasted_iota(jnp.int32, (EXTRA, BLOCK), 1)
        tail = jnp.where(lane < HALF, in_ref[2 * j, HALF:HALF + EXTRA, :].astype(F32),
                         in_ref[2 * j + 1, HALF:HALF + EXTRA, :].astype(F32))
        lines[BLOCK:BLOCK + EXTRA, at] = tail.astype(BF16)
    for j, block in enumerate(run_steps(lines, nb, pow_ref, kta_ref, rb_ref, True)):
        lines[:, j * BLOCK:(j + 1) * BLOCK] = block.astype(BF16)
    for j, block in enumerate(run_steps(lines, nb, pow_ref, ktf_ref, cb_ref, False)):
        square = block[0:BLOCK].T.astype(BF16)
        tail = block[BLOCK:BLOCK + EXTRA].astype(BF16)
        for half in range(2):
            out_ref[2 * j + half, 0:HALF, :] = square[half * HALF:(half + 1) * HALF]
            out_ref[2 * j + half, HALF:HALF + EXTRA, :] = tail


def row_kernel(nb, parity_ref, in_ref, *refs):
    far, out_ref, near, lines, arrived = refs[:7], refs[7], refs[8:15], refs[15], refs[16]
    members_ref, weight_ref, pow_ref, kta_ref, ktf_ref, rb_ref, cb_ref = near
    copies = {id(near[at]): pltpu.make_async_copy(far[at], near[at], arrived.at[at]) for at in range(7)}
    for ref in (kta_ref, pow_ref, rb_ref, ktf_ref, cb_ref, members_ref, weight_ref):
        copies[id(ref)].start()

    def arrive(*wanted):
        for ref in wanted:
            if id(ref) in copies:
                copies.pop(id(ref)).wait()

    shares = in_ref.shape[0]
    for s in range(shares):
        lines[:, s * BLOCK:(s + 1) * BLOCK] = in_ref[s, 0:HALF, :]
    odd = parity_ref[0] == 1
    for half in range(2):
        tail = jnp.concatenate(
            [in_ref[half * 8 + s, HALF:HALF + EXTRA, :] for s in range(8)], axis=0).astype(F32).T
        tail = jnp.where(odd, tail[HALF:BLOCK], tail[0:HALF])
        at = (shares + half) * BLOCK
        lines[:, at:at + BLOCK] = tail.astype(BF16)
    for j, block in enumerate(run_steps(lines, nb, pow_ref, kta_ref, rb_ref, True, arrive)):
        lines[:, j * BLOCK:(j + 1) * BLOCK] = block.astype(BF16)
    takers, middle = out_ref.shape[0], nb // 2
    blocks = run_steps(lines, nb, pow_ref, ktf_ref, cb_ref, False, arrive)
    arrive(members_ref, weight_ref)
    for j in range(middle):
        left, right = slice(j * BLOCK, (j + 1) * BLOCK), slice((middle + j) * BLOCK, (middle + j + 1) * BLOCK)
        term_left = members_ref[0, 0, :, left].astype(F32) * weight_ref[:, left] * blocks[j]
        term_right = members_ref[0, 0, :, right].astype(F32) * weight_ref[:, right] * blocks[middle + j]
        for taker in range(takers):
            rows = slice(taker * 8, taker * 8 + 8)
            out_ref[taker, :, left] = jnp.concatenate([term_left[rows], term_right[rows]], axis=0).astype(BF16)


def sum_kernel(scale, in_ref, out_ref):
    total = in_ref[0].astype(F32)
    for source in range(1, in_ref.shape[0]):
        total += in_ref[source].astype(F32)
    if scale is not None:
        total = total / scale
    total = total.astype(BF16)
    for target in range(out_ref.shape[0]):
        out_ref[target] = total


def final_kernel(mask_ref, in_ref, out_ref):
    shares, _, width = in_ref.shape
    for pair in range(shares // 2):
        one, two = in_ref[2 * pair].astype(F32), in_ref[2 * pair + 1].astype(F32)
        rows = slice(pair * 16, pair * 16 + 16)
        left = jnp.concatenate([one[0:8], two[0:8]], axis=0)
        right = jnp.concatenate([one[8:16], two[8:16]], axis=0)
        out_ref[0, rows, 0:width] = (left * mask_ref[0, rows, 0:width].astype(F32)).astype(BF16)
        out_ref[0, rows, width:2 * width] = (right * mask_ref[0, rows, width:2 * width].astype(F32)).astype(BF16)


def call(kernel, out_shape, operands, scratch=(), spaces=(), limit=VMEM_LIMIT):
    spaces = tuple(spaces) + (pltpu.VMEM,) * (len(operands) - len(spaces))
    return pl.pallas_call(
        kernel,
        out_shape=jax.ShapeDtypeStruct(out_shape, BF16),
        in_specs=[pl.BlockSpec(memory_space=space) for space in spaces],
        out_specs=pl.BlockSpec(memory_space=pltpu.VMEM),
        scratch_shapes=list(scratch),
        compiler_params=pltpu.CompilerParams(vmem_limit_bytes=limit),
        cost_estimate=pl.CostEstimate(flops=1000000, bytes_accessed=2000000, transcendentals=0),
    )(*operands)


def landing(arrays):
    return [pltpu.VMEM(array.shape, array.dtype) for array in arrays], pltpu.SemaphoreType.DMA((len(arrays),))


def exchange(array, axis, groups=None):
    return lax.all_to_all(array, axis, split_axis=0, concat_axis=0, tiled=True, axis_index_groups=groups)


def local(increment, mask, members, weight, x_inverse, x_coupling, y_inverse, y_coupling):
    _, _, rows, columns = members.shape
    space, mem = lax.axis_size("space"), lax.axis_size("mem")
    x_blocks, y_blocks = x_inverse.shape[0], y_inverse.shape[0]
    close = 8
    apart = mem // close
    near_groups = [[z * close + i for i in range(close)] for z in range(apart)]
    far_groups = [[z * close + i for z in range(apart)] for i in range(close)]
    share = (HALF + EXTRA, BLOCK)

    y_tables = prepare(y_inverse, y_coupling, True, False)
    x_tables = prepare(x_inverse, x_coupling, True, True)

    inputs = (increment, mask, members, weight)
    near, arrived = landing(inputs)
    sent = call(start_kernel, (space,) + share, inputs,
                near + [arrived], [pltpu.HBM] * 4, WIDE_LIMIT)
    got = exchange(sent, "space")
    sent = call(functools.partial(column_kernel, y_blocks), (space,) + share, (got,) + tuple(y_tables),
                [pltpu.VMEM((BLOCK + EXTRA, y_blocks * BLOCK), BF16)])
    got = exchange(sent, "space")
    parity = (lax.axis_index("space") % 2).astype(jnp.int32)[None]
    packed = (16, columns // 2)
    inputs = (members, weight) + tuple(x_tables)
    near, arrived = landing(inputs)
    terms = call(functools.partial(row_kernel, x_blocks), (close,) + packed, (parity, got) + inputs,
                 near + [pltpu.VMEM((rows, columns), BF16), arrived],
                 [pltpu.SMEM, pltpu.VMEM] + [pltpu.HBM] * 7, WIDE_LIMIT)
    terms = exchange(terms, "mem", near_groups)
    terms = call(functools.partial(sum_kernel, None), (apart,) + packed, (terms,))
    terms = exchange(terms, "mem", far_groups)
    terms = call(functools.partial(sum_kernel, float(mem - 1)), (close,) + packed, (terms,))
    terms = exchange(terms, "mem", near_groups)
    return call(final_kernel, (1, rows, columns), (mask, terms))


def solution(mesh):
    placed = (
        P(None, "space", None),
        P(None, "space", None),
        P("mem", None, "space", None),
        P("space", None),
        P(),
        P(),
        P(),
        P(),
    )
    return jax.shard_map(
        local, mesh=mesh, in_specs=placed, out_specs=P(None, "space", None), check_vma=False
    )
```

```python
import functools

import jax
import jax.numpy as jnp
from jax import lax
from jax.experimental import pallas as pl
from jax.experimental.pallas import tpu as pltpu
from jax.sharding import PartitionSpec as P


BLOCK = 128
LAST = BLOCK - 1
NSTEP = 7
HALF = 64
EXTRA = 16
F32 = jnp.float32
BF16 = jnp.bfloat16
GROUP = BLOCK // (2 * NSTEP)
VMEM_LIMIT = 24 * 2**20
WIDE_LIMIT = 60 * 2**20


def dot(a, b):
    return lax.dot_general(a, b, (((1,), (0,)), ((), ())), preferred_element_type=F32)


def dot_nt(a, b):
    return lax.dot_general(a, b, (((1,), (1,)), ((), ())), preferred_element_type=F32)


def round_up(value, unit):
    return (value + unit - 1) // unit * unit


def groups_of(nb):
    return (nb + GROUP - 1) // GROUP


def place(j):
    return j // GROUP * BLOCK + j % GROUP * 2 * NSTEP


def prepare_kernel(nb, c_ref, g_ref, pow_ref, map_a_ref, map_f_ref, rows_ref, columns_ref, turned_ref,
                   edges, rows, columns, rmat, qmat, ct, high2, low2, high3, low3, high4, low4,
                   few_rows, few_columns):
    pad = round_up(nb, 8)
    kp = map_a_ref.shape[0]
    lane = lax.broadcasted_iota(jnp.int32, (16, BLOCK), 1)
    row = lax.broadcasted_iota(jnp.int32, (16, BLOCK), 0)
    select = jnp.where((row < 2) & (lane == row * LAST), 1.0, 0.0)
    edges[...] = jnp.zeros_like(edges)
    rows[...] = jnp.zeros_like(rows)
    columns[...] = jnp.zeros_like(columns)

    def stack(first, *pairs):
        out = first
        for at, (top, bottom) in enumerate(pairs):
            out = jnp.where(row == 2 * at + 2, top, jnp.where(row == 2 * at + 3, bottom, out))
        return out.astype(BF16)

    def split(full):
        high = full.astype(BF16)
        return high, (full - high.astype(F32)).astype(BF16)

    def put_row(j, k, top, bottom):
        at = place(j) + 2 * k - 2
        rows[at:at + 1, :] = bottom
        rows[at + 1:at + 2, :] = top
        edges[k - 1, 0, j:j + 1, :] = top
        edges[k - 1, 1, j:j + 1, :] = bottom

    def put_column(j, k, left, right):
        at = place(j) + 2 * k - 2
        columns[at:at + 1, :] = right
        columns[at + 1:at + 2, :] = left

    def ends(full):
        return full[0:1], full[LAST:BLOCK]

    def pair(rows, first):
        return rows[first:first + 1], rows[first + 1:first + 2]

    for j in range(nb):
        g = g_ref[j]
        g_full = g.astype(F32)
        second = dot(g, g)
        high2[j], low2[j] = split(second)
        put_row(j, 1, *ends(g_full))
        put_row(j, 2, *ends(second))
        few_rows[j] = stack(jnp.zeros((16, BLOCK), F32), ends(g_full), ends(second))
        found = dot_nt(select.astype(BF16), g)
        put_column(j, 1, *pair(found, 0))
        few_columns[j] = stack(select, pair(found, 0)).astype(F32)

    for j in range(nb):
        both = jnp.concatenate([g_ref[j], high2[j]], axis=0)
        result = dot(jnp.concatenate([both, both], axis=1), jnp.concatenate([high2[j], low2[j]], axis=0))
        third, fourth = result[0:BLOCK], result[BLOCK:2 * BLOCK] + dot(low2[j], high2[j])
        high3[j], low3[j] = split(third)
        high4[j], low4[j] = split(fourth)
        put_row(j, 3, *ends(third))
        put_row(j, 4, *ends(fourth))
        old = few_columns[j]
        found = dot_nt(old.astype(BF16), high2[j])
        put_column(j, 2, *pair(found, 0))
        put_column(j, 3, *pair(found, 2))
        few_columns[j] = stack(old, pair(old, 2), pair(found, 0), pair(found, 2)).astype(F32)

    for j in range(nb):
        left = jnp.concatenate([high3[j], few_rows[j]], axis=0)
        result = dot(jnp.concatenate([left, left], axis=1), jnp.concatenate([high4[j], low4[j]], axis=0))
        seventh = result[0:BLOCK] + dot(low3[j], high4[j])
        pow_ref[j] = seventh.astype(BF16)
        put_row(j, 5, *pair(result, BLOCK + 2))
        put_row(j, 6, *pair(result, BLOCK + 4))
        put_row(j, 7, *ends(seventh))
        found = dot_nt(few_columns[j].astype(BF16), high4[j])
        for k in range(4):
            put_column(j, 4 + k, *pair(found, 2 * k))

    rows_ref[...] = rows[...].astype(BF16)
    columns_ref[...] = columns[...].astype(BF16)
    for group in range(groups_of(nb)):
        turned_ref[group] = columns[group * BLOCK:(group + 1) * BLOCK, :].T.astype(BF16)

    def corner(run, k, a, b):
        if run == 1:
            a, b = b, a
        return edges[k - 1, a, :, 0:1] if b == 0 else edges[k - 1, a, :, LAST:BLOCK]

    unit = lax.broadcasted_iota(jnp.int32, (1, BLOCK), 1)
    runs = range(2)
    gain_s = [jnp.broadcast_to(corner(run, 1, 0, 1), (pad, BLOCK)) for run in runs]
    gain_t = [jnp.broadcast_to(corner(run, 1, 1, 0), (pad, BLOCK)) for run in runs]
    gain_0 = jnp.broadcast_to(corner(0, 1, 0, 0), (pad, BLOCK))
    rmat[...] = jnp.zeros_like(rmat)
    qmat[...] = jnp.zeros_like(qmat)
    ct[...] = jnp.zeros_like(ct)
    s_row = [jnp.zeros((1, BLOCK), F32) for run in runs]
    p_rows = [[], []]
    for j in range(nb):
        for run in runs:
            p_rows[run].append(jnp.where(unit == pad + j, 1.0, 0.0) + gain_0[j:j + 1] * s_row[run])
            if j + 1 < nb:
                s_row[run] = c_ref[j] * (jnp.where(unit == j, 1.0, 0.0) + gain_s[run][j:j + 1] * s_row[run])
                rmat[run, j + 1:j + 2, :] = s_row[run]
    t_row = [jnp.zeros((1, BLOCK), F32) for run in runs]
    for j in range(nb - 2, -1, -1):
        for run in runs:
            t_row[run] = c_ref[j] * (p_rows[run][j + 1] + gain_t[run][j + 1:j + 2] * t_row[run])
            rmat[run, pad + j:pad + j + 1, :] = t_row[run]

    block = lax.broadcasted_iota(jnp.int32, (pad, kp), 0)
    first = block * (2 * NSTEP)
    for group in range(1, groups_of(nb)):
        first += jnp.where(block >= group * GROUP, BLOCK - GROUP * 2 * NSTEP, 0)
    first = lax.broadcasted_iota(jnp.int32, (pad, kp), 1) - first
    sources, trailing = [[], []], [[], []]
    for k in range(NSTEP):
        for run in runs:
            q_last = jnp.where((block < nb) & (first == 2 * k), 1.0, 0.0)
            q_first = jnp.where((block < nb) & (first == 2 * k + 1), 1.0, 0.0)
            for m in range(k):
                s_old, t_old = sources[run][m], trailing[run][m]
                q_last += corner(run, k - m + 1, 0, 1) * s_old + corner(run, k - m + 1, 1, 1) * t_old
                q_first += corner(run, k - m + 1, 0, 0) * s_old + corner(run, k - m + 1, 1, 0) * t_old
            qmat[run, 0:pad, :] = q_last
            qmat[run, pad:2 * pad, :] = q_first
        for run in runs:
            now = lax.dot_general(rmat[run], qmat[run], (((1,), (0,)), ((), ())),
                                  precision=lax.Precision.HIGHEST, preferred_element_type=F32)
            sources[run].append(now[0:pad])
            trailing[run].append(now[pad:2 * pad])
            for j in range(nb):
                at = place(j) + (NSTEP - 1 - k) * 2
                ct[run, at:at + 1, :] = now[pad + j:pad + j + 1]
                ct[run, at + 1:at + 2, :] = now[j:j + 1]
    map_a_ref[...] = ct[0].astype(BF16)
    map_f_ref[...] = ct[1].astype(BF16)


def prepare(inverse, coupling):
    nb = inverse.shape[0]
    kp, pad = groups_of(nb) * BLOCK, round_up(nb, 8)
    vmem = pl.BlockSpec(memory_space=pltpu.VMEM)
    shapes = [(nb, BLOCK, BLOCK), (kp, kp), (kp, kp), (kp, BLOCK), (kp, BLOCK), (groups_of(nb), BLOCK, BLOCK)]
    return pl.pallas_call(
        functools.partial(prepare_kernel, nb),
        out_shape=tuple(jax.ShapeDtypeStruct(shape, BF16) for shape in shapes),
        in_specs=[pl.BlockSpec(memory_space=pltpu.SMEM), vmem],
        out_specs=(vmem,) * len(shapes),
        scratch_shapes=[
            pltpu.VMEM((NSTEP, 2, pad, BLOCK), F32),
            pltpu.VMEM((kp, BLOCK), F32),
            pltpu.VMEM((kp, BLOCK), F32),
            pltpu.VMEM((2, 2 * pad, BLOCK), F32),
            pltpu.VMEM((2, BLOCK, kp), F32),
            pltpu.VMEM((2, kp, kp), F32),
        ] + [pltpu.VMEM((nb, BLOCK, BLOCK), BF16)] * 6 + [
            pltpu.VMEM((nb, 16, BLOCK), BF16),
            pltpu.VMEM((nb, 16, BLOCK), F32),
        ],
        compiler_params=pltpu.CompilerParams(vmem_limit_bytes=VMEM_LIMIT),
        cost_estimate=pl.CostEstimate(
            flops=nb * 400 * BLOCK**3, bytes_accessed=4000000, transcendentals=0),
    )(coupling, inverse)


def run_steps(lines, nb, pow_ref, map_ref, in_ref, out_ref, adjoint):
    count = lines.shape[0]
    lane = lax.broadcasted_iota(jnp.int32, (count, BLOCK), 1)
    owned = [(lane >= at * 2 * NSTEP) & (lane < (at + 1) * 2 * NSTEP) for at in range(min(nb, GROUP))]
    blocks = [slice(j * BLOCK, (j + 1) * BLOCK) for j in range(nb)]
    products = []
    for group in range(groups_of(nb)):
        edge = in_ref[group * BLOCK:(group + 1) * BLOCK, :]
        kept = jnp.zeros((count, BLOCK), F32)
        for j in range(group * GROUP, min(nb, (group + 1) * GROUP)):
            kept = jnp.where(owned[j % GROUP], dot_nt(lines[:, blocks[j]], edge), kept)
        products.append(kept.astype(BF16))
    coupled = dot_nt(jnp.concatenate(products, axis=1), map_ref[...])
    results = []
    for j in range(nb):
        group = j // GROUP
        mine = jnp.where(owned[j % GROUP], coupled[:, group * BLOCK:(group + 1) * BLOCK], 0.0).astype(BF16)
        left = jnp.concatenate([lines[:, blocks[j]], mine], axis=1)
        if adjoint:
            edge = out_ref[group * BLOCK:(group + 1) * BLOCK, :]
            results.append(dot(left, jnp.concatenate([pow_ref[j], edge], axis=0)))
        else:
            results.append(dot_nt(left, jnp.concatenate([pow_ref[j], out_ref[group]], axis=1)))
    return results


def run_both(lines, nb, pow_ref, map_a_ref, map_f_ref, rows_ref, columns_ref, turned_ref):
    for j, block in enumerate(run_steps(lines, nb, pow_ref, map_a_ref, columns_ref, rows_ref, True)):
        lines[:, j * BLOCK:(j + 1) * BLOCK] = block.astype(BF16)
    return run_steps(lines, nb, pow_ref, map_f_ref, rows_ref, turned_ref, False)


def start_kernel(increment_hbm, mask_hbm, members_hbm, weight_hbm, out_ref,
                 increment_ref, mask_ref, members_ref, weight_ref, arrived):
    copies = [
        pltpu.make_async_copy(source, target, arrived.at[at])
        for at, (source, target) in enumerate((
            (increment_hbm, increment_ref), (mask_hbm, mask_ref),
            (members_hbm, members_ref), (weight_hbm, weight_ref)))
    ]
    for copy in copies:
        copy.start()
    for copy in copies:
        copy.wait()
    shares = out_ref.shape[0]

    def values(at):
        return (weight_ref[:, at] * mask_ref[0, :, at].astype(F32) * members_ref[0, 0, :, at].astype(F32)
                * increment_ref[0, :, at].astype(F32))

    for half in range(2):
        tail = values(slice((shares + half) * BLOCK, (shares + half + 1) * BLOCK))
        turned = jnp.concatenate([tail, tail], axis=0).T
        for s in range(8):
            out_ref[half * 8 + s, HALF:HALF + EXTRA, :] = turned[s * EXTRA:(s + 1) * EXTRA].astype(BF16)
    for s in range(shares):
        out_ref[s, 0:HALF, :] = values(slice(s * BLOCK, (s + 1) * BLOCK)).astype(BF16)


def column_kernel(nb, in_ref, *refs):
    *tables, out_ref, lines = refs
    for j in range(nb):
        at = slice(j * BLOCK, (j + 1) * BLOCK)
        square = jnp.concatenate([in_ref[2 * j, 0:HALF, :], in_ref[2 * j + 1, 0:HALF, :]], axis=0)
        lines[0:BLOCK, at] = square.astype(F32).T.astype(BF16)
        lane = lax.broadcasted_iota(jnp.int32, (EXTRA, BLOCK), 1)
        tail = jnp.where(lane < HALF, in_ref[2 * j, HALF:HALF + EXTRA, :].astype(F32),
                         in_ref[2 * j + 1, HALF:HALF + EXTRA, :].astype(F32))
        lines[BLOCK:BLOCK + EXTRA, at] = tail.astype(BF16)
    for j, block in enumerate(run_both(lines, nb, *tables)):
        square = block[0:BLOCK].T.astype(BF16)
        tail = block[BLOCK:BLOCK + EXTRA].astype(BF16)
        for half in range(2):
            out_ref[2 * j + half, 0:HALF, :] = square[half * HALF:(half + 1) * HALF]
            out_ref[2 * j + half, HALF:HALF + EXTRA, :] = tail


def row_kernel(nb, parity_ref, in_ref, *refs):
    members_hbm, weight_hbm, *tables, out_ref, members_ref, weight_ref, lines, arrived = refs
    copies = [pltpu.make_async_copy(members_hbm, members_ref, arrived.at[0]),
              pltpu.make_async_copy(weight_hbm, weight_ref, arrived.at[1])]
    for copy in copies:
        copy.start()
    shares = in_ref.shape[0]
    for s in range(shares):
        lines[:, s * BLOCK:(s + 1) * BLOCK] = in_ref[s, 0:HALF, :]
    odd = parity_ref[0] == 1
    for half in range(2):
        tail = jnp.concatenate(
            [in_ref[half * 8 + s, HALF:HALF + EXTRA, :] for s in range(8)], axis=0).astype(F32).T
        tail = jnp.where(odd, tail[HALF:BLOCK], tail[0:HALF])
        at = (shares + half) * BLOCK
        lines[:, at:at + BLOCK] = tail.astype(BF16)
    takers, middle = out_ref.shape[0], nb // 2
    blocks = run_both(lines, nb, *tables)
    for copy in copies:
        copy.wait()
    for j in range(middle):
        left, right = slice(j * BLOCK, (j + 1) * BLOCK), slice((middle + j) * BLOCK, (middle + j + 1) * BLOCK)
        term_left = members_ref[0, 0, :, left].astype(F32) * weight_ref[:, left] * blocks[j]
        term_right = members_ref[0, 0, :, right].astype(F32) * weight_ref[:, right] * blocks[middle + j]
        for taker in range(takers):
            rows = slice(taker * 8, taker * 8 + 8)
            out_ref[taker, :, left] = jnp.concatenate([term_left[rows], term_right[rows]], axis=0).astype(BF16)


def sum_kernel(scale, in_ref, out_ref):
    total = in_ref[0].astype(F32)
    for source in range(1, in_ref.shape[0]):
        total += in_ref[source].astype(F32)
    if scale is not None:
        total = total / scale
    total = total.astype(BF16)
    for target in range(out_ref.shape[0]):
        out_ref[target] = total


def final_kernel(mask_ref, in_ref, out_ref):
    shares, _, width = in_ref.shape
    for pair in range(shares // 2):
        one, two = in_ref[2 * pair].astype(F32), in_ref[2 * pair + 1].astype(F32)
        rows = slice(pair * 16, pair * 16 + 16)
        left = jnp.concatenate([one[0:8], two[0:8]], axis=0)
        right = jnp.concatenate([one[8:16], two[8:16]], axis=0)
        out_ref[0, rows, 0:width] = (left * mask_ref[0, rows, 0:width].astype(F32)).astype(BF16)
        out_ref[0, rows, width:2 * width] = (right * mask_ref[0, rows, width:2 * width].astype(F32)).astype(BF16)


def call(kernel, out_shape, operands, scratch=(), spaces=(), limit=VMEM_LIMIT):
    spaces = tuple(spaces) + (pltpu.VMEM,) * (len(operands) - len(spaces))
    return pl.pallas_call(
        kernel,
        out_shape=jax.ShapeDtypeStruct(out_shape, BF16),
        in_specs=[pl.BlockSpec(memory_space=space) for space in spaces],
        out_specs=pl.BlockSpec(memory_space=pltpu.VMEM),
        scratch_shapes=list(scratch),
        compiler_params=pltpu.CompilerParams(vmem_limit_bytes=limit),
        cost_estimate=pl.CostEstimate(flops=1000000, bytes_accessed=2000000, transcendentals=0),
    )(*operands)


def landing(arrays):
    return [pltpu.VMEM(array.shape, array.dtype) for array in arrays], pltpu.SemaphoreType.DMA((len(arrays),))


def exchange(array, axis, groups=None):
    return lax.all_to_all(array, axis, split_axis=0, concat_axis=0, tiled=True, axis_index_groups=groups)


def local(increment, mask, members, weight, x_inverse, x_coupling, y_inverse, y_coupling):
    _, _, rows, columns = members.shape
    space, mem = lax.axis_size("space"), lax.axis_size("mem")
    x_blocks, y_blocks = x_inverse.shape[0], y_inverse.shape[0]
    close = 8
    apart = mem // close
    near_groups = [[z * close + i for i in range(close)] for z in range(apart)]
    far_groups = [[z * close + i for z in range(apart)] for i in range(close)]
    share = (HALF + EXTRA, BLOCK)

    y_tables = prepare(y_inverse, y_coupling)
    x_tables = prepare(x_inverse, x_coupling)

    inputs = (increment, mask, members, weight)
    near, arrived = landing(inputs)
    sent = call(start_kernel, (space,) + share, inputs,
                near + [arrived], [pltpu.HBM] * 4, WIDE_LIMIT)
    got = exchange(sent, "space")
    sent = call(functools.partial(column_kernel, y_blocks), (space,) + share, (got,) + tuple(y_tables),
                [pltpu.VMEM((BLOCK + EXTRA, y_blocks * BLOCK), BF16)])
    got = exchange(sent, "space")
    parity = (lax.axis_index("space") % 2).astype(jnp.int32)[None]
    packed = (16, columns // 2)
    inputs = (members, weight)
    near, arrived = landing(inputs)
    terms = call(functools.partial(row_kernel, x_blocks), (close,) + packed,
                 (parity, got) + inputs + tuple(x_tables),
                 near + [pltpu.VMEM((rows, columns), BF16), arrived],
                 [pltpu.SMEM, pltpu.VMEM, pltpu.HBM, pltpu.HBM], WIDE_LIMIT)
    terms = exchange(terms, "mem", near_groups)
    terms = call(functools.partial(sum_kernel, None), (apart,) + packed, (terms,))
    terms = exchange(terms, "mem", far_groups)
    terms = call(functools.partial(sum_kernel, float(mem - 1)), (close,) + packed, (terms,))
    terms = exchange(terms, "mem", near_groups)
    return call(final_kernel, (1, rows, columns), (mask, terms))


def solution(mesh):
    placed = (
        P(None, "space", None),
        P(None, "space", None),
        P("mem", None, "space", None),
        P("space", None),
        P(),
        P(),
        P(),
        P(),
    )
    return jax.shard_map(
        local, mesh=mesh, in_specs=placed, out_specs=P(None, "space", None), check_vma=False
    )
```

```python
import functools

import jax
import jax.numpy as jnp
from jax import lax
from jax.experimental import pallas as pl
from jax.experimental.pallas import tpu as pltpu
from jax.sharding import PartitionSpec as P


BLOCK = 128
LAST = BLOCK - 1
NSTEP = 7
HALF = 64
EXTRA = 16
F32 = jnp.float32
BF16 = jnp.bfloat16
GROUP = BLOCK // (2 * NSTEP)
VMEM_LIMIT = 16 * 2**20
WIDE_LIMIT = 60 * 2**20


def dot(a, b):
    return lax.dot_general(a, b, (((1,), (0,)), ((), ())), preferred_element_type=F32)


def dot_nt(a, b):
    return lax.dot_general(a, b, (((1,), (1,)), ((), ())), preferred_element_type=F32)


def round_up(value, unit):
    return (value + unit - 1) // unit * unit


def groups_of(nb):
    return (nb + GROUP - 1) // GROUP


def place(j):
    return j // GROUP * BLOCK + j % GROUP * 2 * NSTEP


def prepare_kernel(nb, c_ref, g_ref, pow_ref, map_a_ref, map_f_ref, rows_ref, columns_ref, turned_ref,
                   edges, rows, columns, rmat, qmat, ct, high2, low2, high3, low3, high4, low4,
                   few_rows, few_columns):
    pad = round_up(nb, 8)
    kp = map_a_ref.shape[0]
    lane = lax.broadcasted_iota(jnp.int32, (16, BLOCK), 1)
    row = lax.broadcasted_iota(jnp.int32, (16, BLOCK), 0)
    select = jnp.where((row < 2) & (lane == row * LAST), 1.0, 0.0)
    edges[...] = jnp.zeros_like(edges)
    rows[...] = jnp.zeros_like(rows)
    columns[...] = jnp.zeros_like(columns)

    def stack(first, *pairs):
        out = first
        for at, (top, bottom) in enumerate(pairs):
            out = jnp.where(row == 2 * at + 2, top, jnp.where(row == 2 * at + 3, bottom, out))
        return out.astype(BF16)

    def split(full):
        high = full.astype(BF16)
        return high, (full - high.astype(F32)).astype(BF16)

    def put_row(j, k, top, bottom):
        at = place(j) + 2 * k - 2
        rows[at:at + 1, :] = bottom
        rows[at + 1:at + 2, :] = top
        edges[k - 1, 0, j:j + 1, :] = top
        edges[k - 1, 1, j:j + 1, :] = bottom

    def put_column(j, k, left, right):
        at = place(j) + 2 * k - 2
        columns[at:at + 1, :] = right
        columns[at + 1:at + 2, :] = left

    def ends(full):
        return full[0:1], full[LAST:BLOCK]

    def pair(rows, first):
        return rows[first:first + 1], rows[first + 1:first + 2]

    for j in range(nb):
        g = g_ref[j]
        g_full = g.astype(F32)
        second = dot(g, g)
        high2[j], low2[j] = split(second)
        put_row(j, 1, *ends(g_full))
        put_row(j, 2, *ends(second))
        few_rows[j] = stack(jnp.zeros((16, BLOCK), F32), ends(g_full), ends(second))
        found = dot_nt(select.astype(BF16), g)
        put_column(j, 1, *pair(found, 0))
        few_columns[j] = stack(select, pair(found, 0)).astype(F32)

    for j in range(nb):
        both = jnp.concatenate([g_ref[j], high2[j]], axis=0)
        result = dot(jnp.concatenate([both, both], axis=1), jnp.concatenate([high2[j], low2[j]], axis=0))
        third, fourth = result[0:BLOCK], result[BLOCK:2 * BLOCK] + dot(low2[j], high2[j])
        high3[j], low3[j] = split(third)
        high4[j], low4[j] = split(fourth)
        put_row(j, 3, *ends(third))
        put_row(j, 4, *ends(fourth))
        old = few_columns[j]
        found = dot_nt(old.astype(BF16), high2[j])
        put_column(j, 2, *pair(found, 0))
        put_column(j, 3, *pair(found, 2))
        few_columns[j] = stack(old, pair(old, 2), pair(found, 0), pair(found, 2)).astype(F32)

    for j in range(nb):
        left = jnp.concatenate([high3[j], few_rows[j]], axis=0)
        result = dot(jnp.concatenate([left, left], axis=1), jnp.concatenate([high4[j], low4[j]], axis=0))
        seventh = result[0:BLOCK] + dot(low3[j], high4[j])
        pow_ref[j] = seventh.astype(BF16)
        put_row(j, 5, *pair(result, BLOCK + 2))
        put_row(j, 6, *pair(result, BLOCK + 4))
        put_row(j, 7, *ends(seventh))
        found = dot_nt(few_columns[j].astype(BF16), high4[j])
        for k in range(4):
            put_column(j, 4 + k, *pair(found, 2 * k))

    rows_ref[...] = rows[...].astype(BF16)
    columns_ref[...] = columns[...].astype(BF16)
    for group in range(groups_of(nb)):
        turned_ref[group] = columns[group * BLOCK:(group + 1) * BLOCK, :].T.astype(BF16)

    def corner(run, k, a, b):
        if run == 1:
            a, b = b, a
        return edges[k - 1, a, :, 0:1] if b == 0 else edges[k - 1, a, :, LAST:BLOCK]

    unit = lax.broadcasted_iota(jnp.int32, (1, BLOCK), 1)
    runs = range(2)
    gain_s = [jnp.broadcast_to(corner(run, 1, 0, 1), (pad, BLOCK)) for run in runs]
    gain_t = [jnp.broadcast_to(corner(run, 1, 1, 0), (pad, BLOCK)) for run in runs]
    gain_0 = jnp.broadcast_to(corner(0, 1, 0, 0), (pad, BLOCK))
    rmat[...] = jnp.zeros_like(rmat)
    qmat[...] = jnp.zeros_like(qmat)
    ct[...] = jnp.zeros_like(ct)
    s_row = [jnp.zeros((1, BLOCK), F32) for run in runs]
    p_rows = [[], []]
    for j in range(nb):
        for run in runs:
            p_rows[run].append(jnp.where(unit == pad + j, 1.0, 0.0) + gain_0[j:j + 1] * s_row[run])
            if j + 1 < nb:
                s_row[run] = c_ref[j] * (jnp.where(unit == j, 1.0, 0.0) + gain_s[run][j:j + 1] * s_row[run])
                rmat[run, j + 1:j + 2, :] = s_row[run]
    t_row = [jnp.zeros((1, BLOCK), F32) for run in runs]
    for j in range(nb - 2, -1, -1):
        for run in runs:
            t_row[run] = c_ref[j] * (p_rows[run][j + 1] + gain_t[run][j + 1:j + 2] * t_row[run])
            rmat[run, pad + j:pad + j + 1, :] = t_row[run]

    block = lax.broadcasted_iota(jnp.int32, (pad, kp), 0)
    first = block * (2 * NSTEP)
    for group in range(1, groups_of(nb)):
        first += jnp.where(block >= group * GROUP, BLOCK - GROUP * 2 * NSTEP, 0)
    first = lax.broadcasted_iota(jnp.int32, (pad, kp), 1) - first
    sources, trailing = [[], []], [[], []]
    for k in range(NSTEP):
        for run in runs:
            q_last = jnp.where((block < nb) & (first == 2 * k), 1.0, 0.0)
            q_first = jnp.where((block < nb) & (first == 2 * k + 1), 1.0, 0.0)
            for m in range(k):
                s_old, t_old = sources[run][m], trailing[run][m]
                q_last += corner(run, k - m + 1, 0, 1) * s_old + corner(run, k - m + 1, 1, 1) * t_old
                q_first += corner(run, k - m + 1, 0, 0) * s_old + corner(run, k - m + 1, 1, 0) * t_old
            qmat[run, 0:pad, :] = q_last
            qmat[run, pad:2 * pad, :] = q_first
        for run in runs:
            now = lax.dot_general(rmat[run], qmat[run], (((1,), (0,)), ((), ())),
                                  precision=lax.Precision.HIGHEST, preferred_element_type=F32)
            sources[run].append(now[0:pad])
            trailing[run].append(now[pad:2 * pad])
            for j in range(nb):
                at = place(j) + (NSTEP - 1 - k) * 2
                ct[run, at:at + 1, :] = now[pad + j:pad + j + 1]
                ct[run, at + 1:at + 2, :] = now[j:j + 1]
    map_a_ref[...] = ct[0].astype(BF16)
    map_f_ref[...] = ct[1].astype(BF16)


def prepare(inverse, coupling):
    nb = inverse.shape[0]
    kp, pad = groups_of(nb) * BLOCK, round_up(nb, 8)
    vmem = pl.BlockSpec(memory_space=pltpu.VMEM)
    shapes = [(nb, BLOCK, BLOCK), (kp, kp), (kp, kp), (kp, BLOCK), (kp, BLOCK), (groups_of(nb), BLOCK, BLOCK)]
    return pl.pallas_call(
        functools.partial(prepare_kernel, nb),
        out_shape=tuple(jax.ShapeDtypeStruct(shape, BF16) for shape in shapes),
        in_specs=[pl.BlockSpec(memory_space=pltpu.SMEM), vmem],
        out_specs=(vmem,) * len(shapes),
        scratch_shapes=[
            pltpu.VMEM((NSTEP, 2, pad, BLOCK), F32),
            pltpu.VMEM((kp, BLOCK), F32),
            pltpu.VMEM((kp, BLOCK), F32),
            pltpu.VMEM((2, 2 * pad, BLOCK), F32),
            pltpu.VMEM((2, BLOCK, kp), F32),
            pltpu.VMEM((2, kp, kp), F32),
        ] + [pltpu.VMEM((nb, BLOCK, BLOCK), BF16)] * 6 + [
            pltpu.VMEM((nb, 16, BLOCK), BF16),
            pltpu.VMEM((nb, 16, BLOCK), F32),
        ],
        compiler_params=pltpu.CompilerParams(vmem_limit_bytes=VMEM_LIMIT),
        cost_estimate=pl.CostEstimate(
            flops=nb * 400 * BLOCK**3, bytes_accessed=4000000, transcendentals=0),
    )(coupling, inverse)


def run_steps(lines, nb, pow_ref, map_ref, in_ref, out_ref, adjoint):
    count = lines.shape[0]
    lane = lax.broadcasted_iota(jnp.int32, (count, BLOCK), 1)
    owned = [(lane >= at * 2 * NSTEP) & (lane < (at + 1) * 2 * NSTEP) for at in range(min(nb, GROUP))]
    blocks = [slice(j * BLOCK, (j + 1) * BLOCK) for j in range(nb)]
    products = []
    for group in range(groups_of(nb)):
        edge = in_ref[group * BLOCK:(group + 1) * BLOCK, :]
        kept = jnp.zeros((count, BLOCK), F32)
        mine = range(group * GROUP, min(nb, (group + 1) * GROUP))
        if count < BLOCK:
            stacked = dot_nt(jnp.concatenate([lines[:, blocks[j]] for j in mine], axis=0), edge)
            found = [stacked[at * count:(at + 1) * count] for at in range(len(mine))]
        else:
            found = [dot_nt(lines[:, blocks[j]], edge) for j in mine]
        for at in range(len(mine)):
            kept = jnp.where(owned[at], found[at], kept)
        products.append(kept.astype(BF16))
    coupled = dot_nt(jnp.concatenate(products, axis=1), map_ref[...])
    results = []
    for j in range(nb):
        group = j // GROUP
        mine = jnp.where(owned[j % GROUP], coupled[:, group * BLOCK:(group + 1) * BLOCK], 0.0).astype(BF16)
        left = jnp.concatenate([lines[:, blocks[j]], mine], axis=1)
        if adjoint:
            edge = out_ref[group * BLOCK:(group + 1) * BLOCK, :]
            results.append(dot(left, jnp.concatenate([pow_ref[j], edge], axis=0)))
        else:
            results.append(dot_nt(left, jnp.concatenate([pow_ref[j], out_ref[group]], axis=1)))
    return results


def run_both(lines, nb, pow_ref, map_a_ref, map_f_ref, rows_ref, columns_ref, turned_ref):
    for j, block in enumerate(run_steps(lines, nb, pow_ref, map_a_ref, columns_ref, rows_ref, True)):
        lines[:, j * BLOCK:(j + 1) * BLOCK] = block.astype(BF16)
    return run_steps(lines, nb, pow_ref, map_f_ref, rows_ref, turned_ref, False)


def start_kernel(increment_hbm, mask_hbm, members_hbm, weight_hbm, out_ref,
                 increment_ref, mask_ref, members_ref, weight_ref, arrived):
    copies = [
        pltpu.make_async_copy(source, target, arrived.at[at])
        for at, (source, target) in enumerate((
            (increment_hbm, increment_ref), (mask_hbm, mask_ref),
            (members_hbm, members_ref), (weight_hbm, weight_ref)))
    ]
    for copy in copies:
        copy.start()
    for copy in copies:
        copy.wait()
    shares = out_ref.shape[0]

    def values(at):
        return (weight_ref[:, at] * mask_ref[0, :, at].astype(F32) * members_ref[0, 0, :, at].astype(F32)
                * increment_ref[0, :, at].astype(F32))

    for half in range(2):
        tail = values(slice((shares + half) * BLOCK, (shares + half + 1) * BLOCK))
        turned = jnp.concatenate([tail, tail], axis=0).T
        for s in range(8):
            out_ref[half * 8 + s, HALF:HALF + EXTRA, :] = turned[s * EXTRA:(s + 1) * EXTRA].astype(BF16)
    for s in range(shares):
        out_ref[s, 0:HALF, :] = values(slice(s * BLOCK, (s + 1) * BLOCK)).astype(BF16)


def column_kernel(nb, in_ref, *refs):
    *tables, out_ref, lines = refs
    for j in range(nb):
        at = slice(j * BLOCK, (j + 1) * BLOCK)
        square = jnp.concatenate([in_ref[2 * j, 0:HALF, :], in_ref[2 * j + 1, 0:HALF, :]], axis=0)
        lines[0:BLOCK, at] = square.astype(F32).T.astype(BF16)
        lane = lax.broadcasted_iota(jnp.int32, (EXTRA, BLOCK), 1)
        tail = jnp.where(lane < HALF, in_ref[2 * j, HALF:HALF + EXTRA, :].astype(F32),
                         in_ref[2 * j + 1, HALF:HALF + EXTRA, :].astype(F32))
        lines[BLOCK:BLOCK + EXTRA, at] = tail.astype(BF16)
    for j, block in enumerate(run_both(lines, nb, *tables)):
        square = block[0:BLOCK].T.astype(BF16)
        tail = block[BLOCK:BLOCK + EXTRA].astype(BF16)
        for half in range(2):
            out_ref[2 * j + half, 0:HALF, :] = square[half * HALF:(half + 1) * HALF]
            out_ref[2 * j + half, HALF:HALF + EXTRA, :] = tail


def row_kernel(nb, parity_ref, in_ref, *refs):
    members_hbm, weight_hbm, *tables, out_ref, members_ref, weight_ref, lines, arrived = refs
    copies = [pltpu.make_async_copy(members_hbm, members_ref, arrived.at[0]),
              pltpu.make_async_copy(weight_hbm, weight_ref, arrived.at[1])]
    for copy in copies:
        copy.start()
    shares = in_ref.shape[0]
    for s in range(shares):
        lines[:, s * BLOCK:(s + 1) * BLOCK] = in_ref[s, 0:HALF, :]
    odd = parity_ref[0] == 1
    for half in range(2):
        tail = jnp.concatenate(
            [in_ref[half * 8 + s, HALF:HALF + EXTRA, :] for s in range(8)], axis=0).astype(F32).T
        tail = jnp.where(odd, tail[HALF:BLOCK], tail[0:HALF])
        at = (shares + half) * BLOCK
        lines[:, at:at + BLOCK] = tail.astype(BF16)
    takers, middle = out_ref.shape[0], nb // 2
    blocks = run_both(lines, nb, *tables)
    for copy in copies:
        copy.wait()
    for j in range(middle):
        left, right = slice(j * BLOCK, (j + 1) * BLOCK), slice((middle + j) * BLOCK, (middle + j + 1) * BLOCK)
        term_left = members_ref[0, 0, :, left].astype(F32) * weight_ref[:, left] * blocks[j]
        term_right = members_ref[0, 0, :, right].astype(F32) * weight_ref[:, right] * blocks[middle + j]
        for taker in range(takers):
            rows = slice(taker * 8, taker * 8 + 8)
            out_ref[taker, :, left] = jnp.concatenate([term_left[rows], term_right[rows]], axis=0).astype(BF16)


def sum_kernel(scale, in_ref, out_ref):
    total = in_ref[0].astype(F32)
    for source in range(1, in_ref.shape[0]):
        total += in_ref[source].astype(F32)
    if scale is not None:
        total = total / scale
    total = total.astype(BF16)
    for target in range(out_ref.shape[0]):
        out_ref[target] = total


def add_kernel(scale, one_ref, two_ref, out_ref):
    total = one_ref[0].astype(F32) + two_ref[0].astype(F32)
    if scale is not None:
        total = total / scale
    total = total.astype(BF16)
    for target in range(out_ref.shape[0]):
        out_ref[target] = total


def final_kernel(mask_ref, in_ref, out_ref):
    shares, _, width = in_ref.shape
    for pair in range(shares // 2):
        one, two = in_ref[2 * pair].astype(F32), in_ref[2 * pair + 1].astype(F32)
        rows = slice(pair * 16, pair * 16 + 16)
        left = jnp.concatenate([one[0:8], two[0:8]], axis=0)
        right = jnp.concatenate([one[8:16], two[8:16]], axis=0)
        out_ref[0, rows, 0:width] = (left * mask_ref[0, rows, 0:width].astype(F32)).astype(BF16)
        out_ref[0, rows, width:2 * width] = (right * mask_ref[0, rows, width:2 * width].astype(F32)).astype(BF16)


def call(kernel, out_shape, operands, scratch=(), spaces=(), limit=VMEM_LIMIT):
    spaces = tuple(spaces) + (pltpu.VMEM,) * (len(operands) - len(spaces))
    return pl.pallas_call(
        kernel,
        out_shape=jax.ShapeDtypeStruct(out_shape, BF16),
        in_specs=[pl.BlockSpec(memory_space=space) for space in spaces],
        out_specs=pl.BlockSpec(memory_space=pltpu.VMEM),
        scratch_shapes=list(scratch),
        compiler_params=pltpu.CompilerParams(vmem_limit_bytes=limit),
        cost_estimate=pl.CostEstimate(flops=1000000, bytes_accessed=2000000, transcendentals=0),
    )(*operands)


def landing(arrays):
    return [pltpu.VMEM(array.shape, array.dtype) for array in arrays], pltpu.SemaphoreType.DMA((len(arrays),))


def exchange(array, axis, groups=None):
    return lax.all_to_all(array, axis, split_axis=0, concat_axis=0, tiled=True, axis_index_groups=groups)


def local(increment, mask, members, weight, x_inverse, x_coupling, y_inverse, y_coupling):
    _, _, rows, columns = members.shape
    space, mem = lax.axis_size("space"), lax.axis_size("mem")
    x_blocks, y_blocks = x_inverse.shape[0], y_inverse.shape[0]
    close = 8
    apart = mem // close
    near_groups = [[z * close + i for i in range(close)] for z in range(apart)]
    far_groups = [[z * close + i for z in range(apart)] for i in range(close)]
    share = (HALF + EXTRA, BLOCK)

    y_tables = prepare(y_inverse, y_coupling)
    x_tables = prepare(x_inverse, x_coupling)

    inputs = (increment, mask, members, weight)
    near, arrived = landing(inputs)
    sent = call(start_kernel, (space,) + share, inputs,
                near + [arrived], [pltpu.HBM] * 4, WIDE_LIMIT)
    got = exchange(sent, "space")
    sent = call(functools.partial(column_kernel, y_blocks), (space,) + share, (got,) + tuple(y_tables),
                [pltpu.VMEM((BLOCK + EXTRA, y_blocks * BLOCK), BF16)])
    got = exchange(sent, "space")
    parity = (lax.axis_index("space") % 2).astype(jnp.int32)[None]
    packed = (16, columns // 2)
    inputs = (members, weight)
    near, arrived = landing(inputs)
    terms = call(functools.partial(row_kernel, x_blocks), (close,) + packed,
                 (parity, got) + inputs + tuple(x_tables),
                 near + [pltpu.VMEM((rows, columns), BF16), arrived],
                 [pltpu.SMEM, pltpu.VMEM, pltpu.HBM, pltpu.HBM])
    terms = exchange(terms, "mem", near_groups)
    part = call(functools.partial(sum_kernel, None), (1,) + packed, (terms,))
    for step in range(2):
        pairs = []
        for device in range(mem):
            z, odd = device // close, (device + step) % 2
            pairs.append((device, ((z ^ 1) if odd == 0 else ((z - 1) ^ 1) + 1) % apart * close + device % close))
        other = lax.ppermute(part, "mem", pairs)
        copies, scale = (1, None) if step == 0 else (close, float(mem - 1))
        part = call(functools.partial(add_kernel, scale), (copies,) + packed, (part, other))
    terms = part
    terms = exchange(terms, "mem", near_groups)
    return call(final_kernel, (1, rows, columns), (mask, terms))


def solution(mesh):
    placed = (
        P(None, "space", None),
        P(None, "space", None),
        P("mem", None, "space", None),
        P("space", None),
        P(),
        P(),
        P(),
        P(),
    )
    return jax.shard_map(
        local, mesh=mesh, in_specs=placed, out_specs=P(None, "space", None), check_vma=False
    )
```

```python
import functools

import jax
import jax.numpy as jnp
from jax import lax
from jax.experimental import pallas as pl
from jax.experimental.pallas import tpu as pltpu
from jax.sharding import PartitionSpec as P


BLOCK = 128
LAST = BLOCK - 1
NSTEP = 7
HALF = 64
EXTRA = 16
FOLD = EXTRA // 2
F32 = jnp.float32
BF16 = jnp.bfloat16
GROUP = BLOCK // (2 * NSTEP)
VMEM_LIMIT = 16 * 2**20
WIDE_LIMIT = 60 * 2**20


def dot(a, b):
    return lax.dot_general(a, b, (((1,), (0,)), ((), ())), preferred_element_type=F32)


def dot_nt(a, b):
    return lax.dot_general(a, b, (((1,), (1,)), ((), ())), preferred_element_type=F32)


def round_up(value, unit):
    return (value + unit - 1) // unit * unit


def groups_of(nb):
    return (nb + GROUP - 1) // GROUP


def place(j):
    return j // GROUP * BLOCK + j % GROUP * 2 * NSTEP


def prepare_kernel(nb, c_ref, g_ref, pow_ref, map_a_ref, map_f_ref, rows_ref, columns_ref, turned_ref,
                   edges, rows, columns, rmat, qmat, ct, high2, low2, high3, low3, high4, low4,
                   few_rows, few_columns):
    pad = round_up(nb, 8)
    kp = map_a_ref.shape[0]
    lane = lax.broadcasted_iota(jnp.int32, (16, BLOCK), 1)
    row = lax.broadcasted_iota(jnp.int32, (16, BLOCK), 0)
    select = jnp.where((row < 2) & (lane == row * LAST), 1.0, 0.0)
    edges[...] = jnp.zeros_like(edges)
    rows[...] = jnp.zeros_like(rows)
    columns[...] = jnp.zeros_like(columns)

    def stack(first, *pairs):
        out = first
        for at, (top, bottom) in enumerate(pairs):
            out = jnp.where(row == 2 * at + 2, top, jnp.where(row == 2 * at + 3, bottom, out))
        return out.astype(BF16)

    def split(full):
        high = full.astype(BF16)
        return high, (full - high.astype(F32)).astype(BF16)

    def put_row(j, k, top, bottom):
        at = place(j) + 2 * k - 2
        rows[at:at + 1, :] = bottom
        rows[at + 1:at + 2, :] = top
        edges[k - 1, 0, j:j + 1, :] = top
        edges[k - 1, 1, j:j + 1, :] = bottom

    def put_column(j, k, left, right):
        at = place(j) + 2 * k - 2
        columns[at:at + 1, :] = right
        columns[at + 1:at + 2, :] = left

    def ends(full):
        return full[0:1], full[LAST:BLOCK]

    def pair(rows, first):
        return rows[first:first + 1], rows[first + 1:first + 2]

    for j in range(nb):
        g = g_ref[j]
        g_full = g.astype(F32)
        second = dot(g, g)
        high2[j], low2[j] = split(second)
        put_row(j, 1, *ends(g_full))
        put_row(j, 2, *ends(second))
        few_rows[j] = stack(jnp.zeros((16, BLOCK), F32), ends(g_full), ends(second))
        found = dot_nt(select.astype(BF16), g)
        put_column(j, 1, *pair(found, 0))
        few_columns[j] = stack(select, pair(found, 0)).astype(F32)

    for j in range(nb):
        both = jnp.concatenate([g_ref[j], high2[j]], axis=0)
        result = dot(jnp.concatenate([both, both], axis=1), jnp.concatenate([high2[j], low2[j]], axis=0))
        third, fourth = result[0:BLOCK], result[BLOCK:2 * BLOCK] + dot(low2[j], high2[j])
        high3[j], low3[j] = split(third)
        high4[j], low4[j] = split(fourth)
        put_row(j, 3, *ends(third))
        put_row(j, 4, *ends(fourth))
        old = few_columns[j]
        found = dot_nt(old.astype(BF16), high2[j])
        put_column(j, 2, *pair(found, 0))
        put_column(j, 3, *pair(found, 2))
        few_columns[j] = stack(old, pair(old, 2), pair(found, 0), pair(found, 2)).astype(F32)

    for j in range(nb):
        left = jnp.concatenate([high3[j], few_rows[j]], axis=0)
        result = dot(jnp.concatenate([left, left], axis=1), jnp.concatenate([high4[j], low4[j]], axis=0))
        seventh = result[0:BLOCK] + dot(low3[j], high4[j])
        pow_ref[j] = seventh.astype(BF16)
        put_row(j, 5, *pair(result, BLOCK + 2))
        put_row(j, 6, *pair(result, BLOCK + 4))
        put_row(j, 7, *ends(seventh))
        found = dot_nt(few_columns[j].astype(BF16), high4[j])
        for k in range(4):
            put_column(j, 4 + k, *pair(found, 2 * k))

    rows_ref[...] = rows[...].astype(BF16)
    columns_ref[...] = columns[...].astype(BF16)
    for group in range(groups_of(nb)):
        turned_ref[group] = columns[group * BLOCK:(group + 1) * BLOCK, :].T.astype(BF16)

    def corner(run, k, a, b):
        if run == 1:
            a, b = b, a
        return edges[k - 1, a, :, 0:1] if b == 0 else edges[k - 1, a, :, LAST:BLOCK]

    unit = lax.broadcasted_iota(jnp.int32, (1, BLOCK), 1)
    runs = range(2)
    gain_s = [jnp.broadcast_to(corner(run, 1, 0, 1), (pad, BLOCK)) for run in runs]
    gain_t = [jnp.broadcast_to(corner(run, 1, 1, 0), (pad, BLOCK)) for run in runs]
    gain_0 = jnp.broadcast_to(corner(0, 1, 0, 0), (pad, BLOCK))
    rmat[...] = jnp.zeros_like(rmat)
    qmat[...] = jnp.zeros_like(qmat)
    ct[...] = jnp.zeros_like(ct)
    s_row = [jnp.zeros((1, BLOCK), F32) for run in runs]
    p_rows = [[], []]
    for j in range(nb):
        for run in runs:
            p_rows[run].append(jnp.where(unit == pad + j, 1.0, 0.0) + gain_0[j:j + 1] * s_row[run])
            if j + 1 < nb:
                s_row[run] = c_ref[j] * (jnp.where(unit == j, 1.0, 0.0) + gain_s[run][j:j + 1] * s_row[run])
                rmat[run, j + 1:j + 2, :] = s_row[run]
    t_row = [jnp.zeros((1, BLOCK), F32) for run in runs]
    for j in range(nb - 2, -1, -1):
        for run in runs:
            t_row[run] = c_ref[j] * (p_rows[run][j + 1] + gain_t[run][j + 1:j + 2] * t_row[run])
            rmat[run, pad + j:pad + j + 1, :] = t_row[run]

    block = lax.broadcasted_iota(jnp.int32, (pad, kp), 0)
    first = block * (2 * NSTEP)
    for group in range(1, groups_of(nb)):
        first += jnp.where(block >= group * GROUP, BLOCK - GROUP * 2 * NSTEP, 0)
    first = lax.broadcasted_iota(jnp.int32, (pad, kp), 1) - first
    sources, trailing = [[], []], [[], []]
    for k in range(NSTEP):
        for run in runs:
            q_last = jnp.where((block < nb) & (first == 2 * k), 1.0, 0.0)
            q_first = jnp.where((block < nb) & (first == 2 * k + 1), 1.0, 0.0)
            for m in range(k):
                s_old, t_old = sources[run][m], trailing[run][m]
                q_last += corner(run, k - m + 1, 0, 1) * s_old + corner(run, k - m + 1, 1, 1) * t_old
                q_first += corner(run, k - m + 1, 0, 0) * s_old + corner(run, k - m + 1, 1, 0) * t_old
            qmat[run, 0:pad, :] = q_last
            qmat[run, pad:2 * pad, :] = q_first
        for run in runs:
            now = lax.dot_general(rmat[run], qmat[run], (((1,), (0,)), ((), ())),
                                  precision=lax.Precision.HIGHEST, preferred_element_type=F32)
            sources[run].append(now[0:pad])
            trailing[run].append(now[pad:2 * pad])
            for j in range(nb):
                at = place(j) + (NSTEP - 1 - k) * 2
                ct[run, at:at + 1, :] = now[pad + j:pad + j + 1]
                ct[run, at + 1:at + 2, :] = now[j:j + 1]
    map_a_ref[...] = ct[0].astype(BF16)
    map_f_ref[...] = ct[1].astype(BF16)


def prepare(inverse, coupling):
    nb = inverse.shape[0]
    kp, pad = groups_of(nb) * BLOCK, round_up(nb, 8)
    vmem = pl.BlockSpec(memory_space=pltpu.VMEM)
    shapes = [(nb, BLOCK, BLOCK), (kp, kp), (kp, kp), (kp, BLOCK), (kp, BLOCK), (groups_of(nb), BLOCK, BLOCK)]
    return pl.pallas_call(
        functools.partial(prepare_kernel, nb),
        out_shape=tuple(jax.ShapeDtypeStruct(shape, BF16) for shape in shapes),
        in_specs=[pl.BlockSpec(memory_space=pltpu.SMEM), vmem],
        out_specs=(vmem,) * len(shapes),
        scratch_shapes=[
            pltpu.VMEM((NSTEP, 2, pad, BLOCK), F32),
            pltpu.VMEM((kp, BLOCK), F32),
            pltpu.VMEM((kp, BLOCK), F32),
            pltpu.VMEM((2, 2 * pad, BLOCK), F32),
            pltpu.VMEM((2, BLOCK, kp), F32),
            pltpu.VMEM((2, kp, kp), F32),
        ] + [pltpu.VMEM((nb, BLOCK, BLOCK), BF16)] * 6 + [
            pltpu.VMEM((nb, 16, BLOCK), BF16),
            pltpu.VMEM((nb, 16, BLOCK), F32),
        ],
        compiler_params=pltpu.CompilerParams(vmem_limit_bytes=VMEM_LIMIT),
        cost_estimate=pl.CostEstimate(
            flops=nb * 400 * BLOCK**3, bytes_accessed=4000000, transcendentals=0),
    )(coupling, inverse)


def run_steps(lines, nb, pow_ref, map_ref, in_ref, out_ref, adjoint):
    count = lines.shape[0]
    lane = lax.broadcasted_iota(jnp.int32, (count, BLOCK), 1)
    owned = [(lane >= at * 2 * NSTEP) & (lane < (at + 1) * 2 * NSTEP) for at in range(min(nb, GROUP))]
    blocks = [slice(j * BLOCK, (j + 1) * BLOCK) for j in range(nb)]
    products = []
    for group in range(groups_of(nb)):
        edge = in_ref[group * BLOCK:(group + 1) * BLOCK, :]
        kept = jnp.zeros((count, BLOCK), F32)
        mine = range(group * GROUP, min(nb, (group + 1) * GROUP))
        if count < BLOCK:
            stacked = dot_nt(jnp.concatenate([lines[:, blocks[j]] for j in mine], axis=0), edge)
            found = [stacked[at * count:(at + 1) * count] for at in range(len(mine))]
        else:
            found = [dot_nt(lines[:, blocks[j]], edge) for j in mine]
        for at in range(len(mine)):
            kept = jnp.where(owned[at], found[at], kept)
        products.append(kept.astype(BF16))
    coupled = dot_nt(jnp.concatenate(products, axis=1), map_ref[...])
    results = []
    for j in range(nb):
        group = j // GROUP
        mine = jnp.where(owned[j % GROUP], coupled[:, group * BLOCK:(group + 1) * BLOCK], 0.0).astype(BF16)
        left = jnp.concatenate([lines[:, blocks[j]], mine], axis=1)
        if adjoint:
            edge = out_ref[group * BLOCK:(group + 1) * BLOCK, :]
            results.append(dot(left, jnp.concatenate([pow_ref[j], edge], axis=0)))
        else:
            results.append(dot_nt(left, jnp.concatenate([pow_ref[j], out_ref[group]], axis=1)))
    return results


def run_both(lines, nb, pow_ref, map_a_ref, map_f_ref, rows_ref, columns_ref, turned_ref):
    for j, block in enumerate(run_steps(lines, nb, pow_ref, map_a_ref, columns_ref, rows_ref, True)):
        lines[:, j * BLOCK:(j + 1) * BLOCK] = block.astype(BF16)
    return run_steps(lines, nb, pow_ref, map_f_ref, rows_ref, turned_ref, False)


def beside(left, right):
    return jnp.where(lax.broadcasted_iota(jnp.int32, left.shape, 1) < HALF, left, right)


def swap(tile):
    return pltpu.roll(tile, HALF, 1)


def start_kernel(increment_hbm, mask_hbm, members_hbm, weight_hbm, out_ref,
                 increment_ref, mask_ref, members_ref, weight_ref, arrived):
    copies = [
        pltpu.make_async_copy(source, target, arrived.at[at])
        for at, (source, target) in enumerate((
            (increment_hbm, increment_ref), (mask_hbm, mask_ref),
            (members_hbm, members_ref), (weight_hbm, weight_ref)))
    ]
    for copy in copies:
        copy.start()
    for copy in copies:
        copy.wait()
    shares = out_ref.shape[0]

    def values(at):
        return (weight_ref[:, at] * mask_ref[0, :, at].astype(F32) * members_ref[0, 0, :, at].astype(F32)
                * increment_ref[0, :, at].astype(F32))

    for half in range(2):
        tail = values(slice((shares + half) * BLOCK, (shares + half + 1) * BLOCK))
        turned = jnp.concatenate([tail, tail], axis=0).T
        for s in range(8):
            out_ref[half * 8 + s, HALF:HALF + FOLD, :] = beside(
                turned[s * EXTRA:s * EXTRA + FOLD], turned[s * EXTRA + FOLD:(s + 1) * EXTRA]).astype(BF16)
    for s in range(shares):
        out_ref[s, 0:HALF, :] = values(slice(s * BLOCK, (s + 1) * BLOCK)).astype(BF16)


def column_kernel(nb, in_ref, *refs):
    *tables, out_ref, lines = refs
    for j in range(nb):
        at = slice(j * BLOCK, (j + 1) * BLOCK)
        square = jnp.concatenate([in_ref[2 * j, 0:HALF, :], in_ref[2 * j + 1, 0:HALF, :]], axis=0)
        lines[0:BLOCK, at] = square.astype(F32).T.astype(BF16)
        even = in_ref[2 * j, HALF:HALF + FOLD, :].astype(F32)
        odd = in_ref[2 * j + 1, HALF:HALF + FOLD, :].astype(F32)
        tail = jnp.concatenate([beside(even, swap(odd)), beside(swap(even), odd)], axis=0)
        lines[BLOCK:BLOCK + EXTRA, at] = tail.astype(BF16)
    for j, block in enumerate(run_both(lines, nb, *tables)):
        square = block[0:BLOCK].T.astype(BF16)
        top, bottom = block[BLOCK:BLOCK + FOLD], block[BLOCK + FOLD:BLOCK + EXTRA]
        tails = beside(top, swap(bottom)), beside(swap(top), bottom)
        for half in range(2):
            out_ref[2 * j + half, 0:HALF, :] = square[half * HALF:(half + 1) * HALF]
            out_ref[2 * j + half, HALF:HALF + FOLD, :] = tails[half].astype(BF16)


def row_kernel(nb, in_ref, *refs):
    members_hbm, weight_hbm, *tables, out_ref, members_ref, weight_ref, lines, arrived = refs
    copies = [pltpu.make_async_copy(members_hbm, members_ref, arrived.at[0]),
              pltpu.make_async_copy(weight_hbm, weight_ref, arrived.at[1])]
    for copy in copies:
        copy.start()
    shares = in_ref.shape[0]
    for s in range(shares):
        lines[:, s * BLOCK:(s + 1) * BLOCK] = in_ref[s, 0:HALF, :]
    for half in range(2):
        folded = [in_ref[half * 8 + s, HALF:HALF + FOLD, :].astype(F32) for s in range(8)]
        tail = jnp.concatenate([part for tile in folded for part in (tile, swap(tile))], axis=0).T[0:HALF]
        at = (shares + half) * BLOCK
        lines[:, at:at + BLOCK] = tail.astype(BF16)
    blocks = run_both(lines, nb, *tables)
    for copy in copies:
        copy.wait()
    for j in range(nb):
        at = slice(j * BLOCK, (j + 1) * BLOCK)
        term = members_ref[0, 0, :, at].astype(F32) * weight_ref[:, at] * blocks[j]
        for taker in range(out_ref.shape[0]):
            out_ref[taker, :, at] = term[taker * 8:taker * 8 + 8].astype(BF16)


def sum_kernel(in_ref, out_ref):
    total = in_ref[0].astype(F32)
    for source in range(1, in_ref.shape[0]):
        total += in_ref[source].astype(F32)
    out_ref[0] = total.astype(BF16)


def add_kernel(one_ref, two_ref, out_ref):
    out_ref[0] = (one_ref[0].astype(F32) + two_ref[0].astype(F32)).astype(BF16)


def final_kernel(scale, own_ref, one_ref, two_ref, mask_ref, out_ref):
    rows = out_ref.shape[1]
    mask = mask_ref[0, pl.ds(pl.multiple_of(own_ref[0] * rows, rows), rows), :].astype(F32)
    total = (mask * (one_ref[0].astype(F32) + two_ref[0].astype(F32)) / scale).astype(BF16)
    for target in range(out_ref.shape[0]):
        out_ref[target] = total


def call(kernel, out_shape, operands, scratch=(), spaces=(), limit=VMEM_LIMIT):
    spaces = tuple(spaces) + (pltpu.VMEM,) * (len(operands) - len(spaces))
    return pl.pallas_call(
        kernel,
        out_shape=jax.ShapeDtypeStruct(out_shape, BF16),
        in_specs=[pl.BlockSpec(memory_space=space) for space in spaces],
        out_specs=pl.BlockSpec(memory_space=pltpu.VMEM),
        scratch_shapes=list(scratch),
        compiler_params=pltpu.CompilerParams(vmem_limit_bytes=limit),
        cost_estimate=pl.CostEstimate(flops=1000000, bytes_accessed=2000000, transcendentals=0),
    )(*operands)


def landing(arrays):
    return [pltpu.VMEM(array.shape, array.dtype) for array in arrays], pltpu.SemaphoreType.DMA((len(arrays),))


def exchange(array, axis, groups=None):
    return lax.all_to_all(array, axis, split_axis=0, concat_axis=0, tiled=True, axis_index_groups=groups)


def local(increment, mask, members, weight, x_inverse, x_coupling, y_inverse, y_coupling):
    _, _, rows, columns = members.shape
    space, mem = lax.axis_size("space"), lax.axis_size("mem")
    x_blocks, y_blocks = x_inverse.shape[0], y_inverse.shape[0]
    close = 8
    apart = mem // close
    near_groups = [[z * close + i for i in range(close)] for z in range(apart)]
    far_groups = [[z * close + i for z in range(apart)] for i in range(close)]
    share = (HALF + FOLD, BLOCK)

    y_tables = prepare(y_inverse, y_coupling)
    x_tables = prepare(x_inverse, x_coupling)

    inputs = (increment, mask, members, weight)
    near, arrived = landing(inputs)
    sent = call(start_kernel, (space,) + share, inputs,
                near + [arrived], [pltpu.HBM] * 4, WIDE_LIMIT)
    got = exchange(sent, "space")
    sent = call(functools.partial(column_kernel, y_blocks), (space,) + share, (got,) + tuple(y_tables),
                [pltpu.VMEM((BLOCK + EXTRA, y_blocks * BLOCK), BF16)])
    got = exchange(sent, "space")
    own = (lax.axis_index("mem") % close).astype(jnp.int32)[None]
    packed = (rows // close, columns)
    inputs = (members, weight)
    near, arrived = landing(inputs)
    terms = call(functools.partial(row_kernel, x_blocks), (close,) + packed,
                 (got,) + inputs + tuple(x_tables),
                 near + [pltpu.VMEM((rows, columns), BF16), arrived],
                 [pltpu.VMEM, pltpu.HBM, pltpu.HBM])
    terms = exchange(terms, "mem", near_groups)
    part = call(sum_kernel, (1,) + packed, (terms,))
    for step in range(2):
        pairs = []
        for device in range(mem):
            z, odd = device // close, (device + step) % 2
            pairs.append((device, ((z ^ 1) if odd == 0 else ((z - 1) ^ 1) + 1) % apart * close + device % close))
        other = lax.ppermute(part, "mem", pairs)
        if step == 0:
            part = call(add_kernel, (1,) + packed, (part, other))
    result = call(functools.partial(final_kernel, float(mem - 1)), (close,) + packed, (own, part, other, mask),
                  spaces=[pltpu.SMEM])
    return exchange(result, "mem", near_groups).reshape(1, rows, columns)


def solution(mesh):
    placed = (
        P(None, "space", None),
        P(None, "space", None),
        P("mem", None, "space", None),
        P("space", None),
        P(),
        P(),
        P(),
        P(),
    )
    return jax.shard_map(
        local, mesh=mesh, in_specs=placed, out_specs=P(None, "space", None), check_vma=False
    )
```

```python
import functools

import jax
import jax.numpy as jnp
from jax import lax
from jax.experimental import pallas as pl
from jax.experimental.pallas import tpu as pltpu
from jax.sharding import PartitionSpec as P


BLOCK = 128
LAST = BLOCK - 1
NSTEP = 7
HALF = 64
EXTRA = 16
FOLD = EXTRA // 2
F32 = jnp.float32
BF16 = jnp.bfloat16
GROUP = BLOCK // (2 * NSTEP)
VMEM_LIMIT = 16 * 2**20
WIDE_LIMIT = 60 * 2**20


def dot(a, b):
    return lax.dot_general(a, b, (((1,), (0,)), ((), ())), preferred_element_type=F32)


def dot_nt(a, b):
    return lax.dot_general(a, b, (((1,), (1,)), ((), ())), preferred_element_type=F32)


def round_up(value, unit):
    return (value + unit - 1) // unit * unit


def groups_of(nb):
    return (nb + GROUP - 1) // GROUP


def place(j):
    return j // GROUP * BLOCK + j % GROUP * 2 * NSTEP


def prepare_kernel(nb, c_ref, g_ref, pow_ref, map_a_ref, map_f_ref, rows_ref, columns_ref, turned_ref,
                   edges, rows, columns, rmat, qmat, ct, high2, low2, high3, low3, high4, low4,
                   few_rows, few_columns):
    pad = round_up(nb, 8)
    kp = map_a_ref.shape[0]
    lane = lax.broadcasted_iota(jnp.int32, (16, BLOCK), 1)
    row = lax.broadcasted_iota(jnp.int32, (16, BLOCK), 0)
    select = jnp.where((row < 2) & (lane == row * LAST), 1.0, 0.0)
    edges[...] = jnp.zeros_like(edges)
    rows[...] = jnp.zeros_like(rows)
    columns[...] = jnp.zeros_like(columns)

    def stack(first, *pairs):
        out = first
        for at, (top, bottom) in enumerate(pairs):
            out = jnp.where(row == 2 * at + 2, top, jnp.where(row == 2 * at + 3, bottom, out))
        return out.astype(BF16)

    def split(full):
        high = full.astype(BF16)
        return high, (full - high.astype(F32)).astype(BF16)

    def put_row(j, k, top, bottom):
        at = place(j) + 2 * k - 2
        rows[at:at + 1, :] = bottom
        rows[at + 1:at + 2, :] = top
        edges[k - 1, 0, j:j + 1, :] = top
        edges[k - 1, 1, j:j + 1, :] = bottom

    def put_column(j, k, left, right):
        at = place(j) + 2 * k - 2
        columns[at:at + 1, :] = right
        columns[at + 1:at + 2, :] = left

    def ends(full):
        return full[0:1], full[LAST:BLOCK]

    def pair(rows, first):
        return rows[first:first + 1], rows[first + 1:first + 2]

    for j in range(nb):
        g = g_ref[j]
        g_full = g.astype(F32)
        second = dot(g, g)
        high2[j], low2[j] = split(second)
        put_row(j, 1, *ends(g_full))
        put_row(j, 2, *ends(second))
        few_rows[j] = stack(jnp.zeros((16, BLOCK), F32), ends(g_full), ends(second))
        found = dot_nt(select.astype(BF16), g)
        put_column(j, 1, *pair(found, 0))
        few_columns[j] = stack(select, pair(found, 0)).astype(F32)

    for j in range(nb):
        both = jnp.concatenate([g_ref[j], high2[j]], axis=0)
        result = dot(jnp.concatenate([both, both], axis=1), jnp.concatenate([high2[j], low2[j]], axis=0))
        third, fourth = result[0:BLOCK], result[BLOCK:2 * BLOCK] + dot(low2[j], high2[j])
        high3[j], low3[j] = split(third)
        high4[j], low4[j] = split(fourth)
        put_row(j, 3, *ends(third))
        put_row(j, 4, *ends(fourth))
        old = few_columns[j]
        found = dot_nt(old.astype(BF16), high2[j])
        put_column(j, 2, *pair(found, 0))
        put_column(j, 3, *pair(found, 2))
        few_columns[j] = stack(old, pair(old, 2), pair(found, 0), pair(found, 2)).astype(F32)

    for j in range(nb):
        left = jnp.concatenate([high3[j], few_rows[j]], axis=0)
        result = dot(jnp.concatenate([left, left], axis=1), jnp.concatenate([high4[j], low4[j]], axis=0))
        seventh = result[0:BLOCK] + dot(low3[j], high4[j])
        pow_ref[j] = seventh.astype(BF16)
        put_row(j, 5, *pair(result, BLOCK + 2))
        put_row(j, 6, *pair(result, BLOCK + 4))
        put_row(j, 7, *ends(seventh))
        found = dot_nt(few_columns[j].astype(BF16), high4[j])
        for k in range(4):
            put_column(j, 4 + k, *pair(found, 2 * k))

    rows_ref[...] = rows[...].astype(BF16)
    columns_ref[...] = columns[...].astype(BF16)
    for group in range(groups_of(nb)):
        turned_ref[group] = columns[group * BLOCK:(group + 1) * BLOCK, :].T.astype(BF16)

    def corner(run, k, a, b):
        if run == 1:
            a, b = b, a
        return edges[k - 1, a, :, 0:1] if b == 0 else edges[k - 1, a, :, LAST:BLOCK]

    unit = lax.broadcasted_iota(jnp.int32, (1, BLOCK), 1)
    runs = range(2)
    gain_s = [jnp.broadcast_to(corner(run, 1, 0, 1), (pad, BLOCK)) for run in runs]
    gain_t = [jnp.broadcast_to(corner(run, 1, 1, 0), (pad, BLOCK)) for run in runs]
    gain_0 = jnp.broadcast_to(corner(0, 1, 0, 0), (pad, BLOCK))
    rmat[...] = jnp.zeros_like(rmat)
    qmat[...] = jnp.zeros_like(qmat)
    ct[...] = jnp.zeros_like(ct)
    s_row = [jnp.zeros((1, BLOCK), F32) for run in runs]
    p_rows = [[], []]
    for j in range(nb):
        for run in runs:
            p_rows[run].append(jnp.where(unit == pad + j, 1.0, 0.0) + gain_0[j:j + 1] * s_row[run])
            if j + 1 < nb:
                s_row[run] = c_ref[j] * (jnp.where(unit == j, 1.0, 0.0) + gain_s[run][j:j + 1] * s_row[run])
                rmat[run, j + 1:j + 2, :] = s_row[run]
    t_row = [jnp.zeros((1, BLOCK), F32) for run in runs]
    for j in range(nb - 2, -1, -1):
        for run in runs:
            t_row[run] = c_ref[j] * (p_rows[run][j + 1] + gain_t[run][j + 1:j + 2] * t_row[run])
            rmat[run, pad + j:pad + j + 1, :] = t_row[run]

    block = lax.broadcasted_iota(jnp.int32, (pad, kp), 0)
    first = block * (2 * NSTEP)
    for group in range(1, groups_of(nb)):
        first += jnp.where(block >= group * GROUP, BLOCK - GROUP * 2 * NSTEP, 0)
    first = lax.broadcasted_iota(jnp.int32, (pad, kp), 1) - first
    sources, trailing = [[], []], [[], []]
    for k in range(NSTEP):
        for run in runs:
            q_last = jnp.where((block < nb) & (first == 2 * k), 1.0, 0.0)
            q_first = jnp.where((block < nb) & (first == 2 * k + 1), 1.0, 0.0)
            for m in range(k):
                s_old, t_old = sources[run][m], trailing[run][m]
                q_last += corner(run, k - m + 1, 0, 1) * s_old + corner(run, k - m + 1, 1, 1) * t_old
                q_first += corner(run, k - m + 1, 0, 0) * s_old + corner(run, k - m + 1, 1, 0) * t_old
            qmat[run, 0:pad, :] = q_last
            qmat[run, pad:2 * pad, :] = q_first
        for run in runs:
            now = lax.dot_general(rmat[run], qmat[run], (((1,), (0,)), ((), ())),
                                  precision=lax.Precision.HIGHEST, preferred_element_type=F32)
            sources[run].append(now[0:pad])
            trailing[run].append(now[pad:2 * pad])
            for j in range(nb):
                at = place(j) + (NSTEP - 1 - k) * 2
                ct[run, at:at + 1, :] = now[pad + j:pad + j + 1]
                ct[run, at + 1:at + 2, :] = now[j:j + 1]
    map_a_ref[...] = ct[0].astype(BF16)
    map_f_ref[...] = ct[1].astype(BF16)


def prepare(inverse, coupling):
    nb = inverse.shape[0]
    kp, pad = groups_of(nb) * BLOCK, round_up(nb, 8)
    vmem = pl.BlockSpec(memory_space=pltpu.VMEM)
    shapes = [(nb, BLOCK, BLOCK), (kp, kp), (kp, kp), (kp, BLOCK), (kp, BLOCK), (groups_of(nb), BLOCK, BLOCK)]
    return pl.pallas_call(
        functools.partial(prepare_kernel, nb),
        out_shape=tuple(jax.ShapeDtypeStruct(shape, BF16) for shape in shapes),
        in_specs=[pl.BlockSpec(memory_space=pltpu.SMEM), vmem],
        out_specs=(vmem,) * len(shapes),
        scratch_shapes=[
            pltpu.VMEM((NSTEP, 2, pad, BLOCK), F32),
            pltpu.VMEM((kp, BLOCK), F32),
            pltpu.VMEM((kp, BLOCK), F32),
            pltpu.VMEM((2, 2 * pad, BLOCK), F32),
            pltpu.VMEM((2, BLOCK, kp), F32),
            pltpu.VMEM((2, kp, kp), F32),
        ] + [pltpu.VMEM((nb, BLOCK, BLOCK), BF16)] * 6 + [
            pltpu.VMEM((nb, 16, BLOCK), BF16),
            pltpu.VMEM((nb, 16, BLOCK), F32),
        ],
        compiler_params=pltpu.CompilerParams(vmem_limit_bytes=VMEM_LIMIT),
        cost_estimate=pl.CostEstimate(
            flops=nb * 400 * BLOCK**3, bytes_accessed=4000000, transcendentals=0),
    )(coupling, inverse)


def run_steps(lines, nb, pow_ref, map_ref, in_ref, out_ref, adjoint):
    count = lines.shape[0]
    lane = lax.broadcasted_iota(jnp.int32, (count, BLOCK), 1)
    owned = [(lane >= at * 2 * NSTEP) & (lane < (at + 1) * 2 * NSTEP) for at in range(min(nb, GROUP))]
    blocks = [slice(j * BLOCK, (j + 1) * BLOCK) for j in range(nb)]
    products = []
    for group in range(groups_of(nb)):
        edge = in_ref[group * BLOCK:(group + 1) * BLOCK, :]
        kept = jnp.zeros((count, BLOCK), F32)
        mine = range(group * GROUP, min(nb, (group + 1) * GROUP))
        if count < BLOCK:
            stacked = dot_nt(jnp.concatenate([lines[:, blocks[j]] for j in mine], axis=0), edge)
            found = [stacked[at * count:(at + 1) * count] for at in range(len(mine))]
        else:
            found = [dot_nt(lines[:, blocks[j]], edge) for j in mine]
        for at in range(len(mine)):
            kept = jnp.where(owned[at], found[at], kept)
        products.append(kept.astype(BF16))
    coupled = dot_nt(jnp.concatenate(products, axis=1), map_ref[...])
    results = []
    for j in range(nb):
        group = j // GROUP
        mine = jnp.where(owned[j % GROUP], coupled[:, group * BLOCK:(group + 1) * BLOCK], 0.0).astype(BF16)
        left = jnp.concatenate([lines[:, blocks[j]], mine], axis=1)
        if adjoint:
            edge = out_ref[group * BLOCK:(group + 1) * BLOCK, :]
            results.append(dot(left, jnp.concatenate([pow_ref[j], edge], axis=0)))
        else:
            results.append(dot_nt(left, jnp.concatenate([pow_ref[j], out_ref[group]], axis=1)))
    return results


def run_both(lines, nb, pow_ref, map_a_ref, map_f_ref, rows_ref, columns_ref, turned_ref):
    for j, block in enumerate(run_steps(lines, nb, pow_ref, map_a_ref, columns_ref, rows_ref, True)):
        lines[:, j * BLOCK:(j + 1) * BLOCK] = block.astype(BF16)
    return run_steps(lines, nb, pow_ref, map_f_ref, rows_ref, turned_ref, False)


def beside(left, right):
    return jnp.where(lax.broadcasted_iota(jnp.int32, left.shape, 1) < HALF, left, right)


def swap(tile):
    return pltpu.roll(tile, HALF, 1)


def start_kernel(increment_hbm, mask_hbm, members_hbm, weight_hbm, out_ref,
                 increment_ref, mask_ref, members_ref, weight_ref, arrived):
    copies = [
        pltpu.make_async_copy(source, target, arrived.at[at])
        for at, (source, target) in enumerate((
            (increment_hbm, increment_ref), (mask_hbm, mask_ref),
            (members_hbm, members_ref), (weight_hbm, weight_ref)))
    ]
    for copy in copies:
        copy.start()
    for copy in copies:
        copy.wait()
    shares = out_ref.shape[0]

    def values(at):
        return (weight_ref[:, at] * mask_ref[0, :, at].astype(F32) * members_ref[0, 0, :, at].astype(F32)
                * increment_ref[0, :, at].astype(F32))

    for half in range(2):
        tail = values(slice((shares + half) * BLOCK, (shares + half + 1) * BLOCK))
        turned = jnp.concatenate([tail, tail], axis=0).T
        for s in range(8):
            out_ref[half * 8 + s, HALF:HALF + FOLD, :] = beside(
                turned[s * EXTRA:s * EXTRA + FOLD], turned[s * EXTRA + FOLD:(s + 1) * EXTRA]).astype(BF16)
    for s in range(shares):
        out_ref[s, 0:HALF, :] = values(slice(s * BLOCK, (s + 1) * BLOCK)).astype(BF16)


def column_kernel(nb, in_ref, *refs):
    *tables, out_ref, lines = refs
    for j in range(nb):
        at = slice(j * BLOCK, (j + 1) * BLOCK)
        square = jnp.concatenate([in_ref[2 * j, 0:HALF, :], in_ref[2 * j + 1, 0:HALF, :]], axis=0)
        lines[0:BLOCK, at] = square.astype(F32).T.astype(BF16)
        even = in_ref[2 * j, HALF:HALF + FOLD, :].astype(F32)
        odd = in_ref[2 * j + 1, HALF:HALF + FOLD, :].astype(F32)
        tail = jnp.concatenate([beside(even, swap(odd)), beside(swap(even), odd)], axis=0)
        lines[BLOCK:BLOCK + EXTRA, at] = tail.astype(BF16)
    for j, block in enumerate(run_both(lines, nb, *tables)):
        square = block[0:BLOCK].T.astype(BF16)
        top, bottom = block[BLOCK:BLOCK + FOLD], block[BLOCK + FOLD:BLOCK + EXTRA]
        tails = beside(top, swap(bottom)), beside(swap(top), bottom)
        for half in range(2):
            out_ref[2 * j + half, 0:HALF, :] = square[half * HALF:(half + 1) * HALF]
            out_ref[2 * j + half, HALF:HALF + FOLD, :] = tails[half].astype(BF16)


def row_kernel(nb, in_ref, *refs):
    members_hbm, weight_hbm, *tables, out_ref, members_ref, weight_ref, lines, arrived = refs
    copies = [pltpu.make_async_copy(members_hbm, members_ref, arrived.at[0]),
              pltpu.make_async_copy(weight_hbm, weight_ref, arrived.at[1])]
    for copy in copies:
        copy.start()
    shares = in_ref.shape[0]
    for s in range(shares):
        lines[:, s * BLOCK:(s + 1) * BLOCK] = in_ref[s, 0:HALF, :]
    for half in range(2):
        folded = [in_ref[half * 8 + s, HALF:HALF + FOLD, :].astype(F32) for s in range(8)]
        tail = jnp.concatenate([part for tile in folded for part in (tile, swap(tile))], axis=0).T[0:HALF]
        at = (shares + half) * BLOCK
        lines[:, at:at + BLOCK] = tail.astype(BF16)
    blocks = run_both(lines, nb, *tables)
    for copy in copies:
        copy.wait()
    for j in range(nb):
        at = slice(j * BLOCK, (j + 1) * BLOCK)
        term = members_ref[0, 0, :, at].astype(F32) * weight_ref[:, at] * blocks[j]
        half, at = j // (nb // 2), slice(j % (nb // 2) * BLOCK, (j % (nb // 2) + 1) * BLOCK)
        for taker in range(out_ref.shape[0] // 2):
            out_ref[2 * taker + half, :, at] = term[taker * 8:taker * 8 + 8].astype(BF16)


def sum_kernel(in_ref, out_ref):
    total = in_ref[0].astype(F32)
    for source in range(1, in_ref.shape[0]):
        total += in_ref[source].astype(F32)
    out_ref[0] = total.astype(BF16)


def add_kernel(scale, one_ref, two_ref, out_ref):
    total = ((one_ref[0].astype(F32) + two_ref[0].astype(F32)) / scale).astype(BF16)
    for target in range(out_ref.shape[0]):
        out_ref[target] = total


def final_kernel(mask_ref, in_ref, out_ref):
    width = in_ref.shape[2]
    for group in range(in_ref.shape[0] // 4):
        rows = slice(group * 16, group * 16 + 16)
        for half in range(2):
            at = slice(half * width, (half + 1) * width)
            part = jnp.concatenate([in_ref[4 * group + half].astype(F32), in_ref[4 * group + 2 + half].astype(F32)], axis=0)
            out_ref[0, rows, at] = (part * mask_ref[0, rows, at].astype(F32)).astype(BF16)


def call(kernel, out_shape, operands, scratch=(), spaces=(), limit=VMEM_LIMIT):
    spaces = tuple(spaces) + (pltpu.VMEM,) * (len(operands) - len(spaces))
    return pl.pallas_call(
        kernel,
        out_shape=jax.ShapeDtypeStruct(out_shape, BF16),
        in_specs=[pl.BlockSpec(memory_space=space) for space in spaces],
        out_specs=pl.BlockSpec(memory_space=pltpu.VMEM),
        scratch_shapes=list(scratch),
        compiler_params=pltpu.CompilerParams(vmem_limit_bytes=limit),
        cost_estimate=pl.CostEstimate(flops=1000000, bytes_accessed=2000000, transcendentals=0),
    )(*operands)


def landing(arrays):
    return [pltpu.VMEM(array.shape, array.dtype) for array in arrays], pltpu.SemaphoreType.DMA((len(arrays),))


def exchange(array, axis, groups=None):
    return lax.all_to_all(array, axis, split_axis=0, concat_axis=0, tiled=True, axis_index_groups=groups)


def local(increment, mask, members, weight, x_inverse, x_coupling, y_inverse, y_coupling):
    _, _, rows, columns = members.shape
    space, mem = lax.axis_size("space"), lax.axis_size("mem")
    x_blocks, y_blocks = x_inverse.shape[0], y_inverse.shape[0]
    close = 8
    half = mem // 2
    halves = [list(range(half)), list(range(mem - close, mem)) + list(range(half, mem - close))]
    twins = [(device, mem - close - device // close * close + device % close) for device in range(mem)]
    share = (HALF + FOLD, BLOCK)

    y_tables = prepare(y_inverse, y_coupling)
    x_tables = prepare(x_inverse, x_coupling)

    inputs = (increment, mask, members, weight)
    near, arrived = landing(inputs)
    sent = call(start_kernel, (space,) + share, inputs,
                near + [arrived], [pltpu.HBM] * 4, WIDE_LIMIT)
    got = exchange(sent, "space")
    sent = call(functools.partial(column_kernel, y_blocks), (space,) + share, (got,) + tuple(y_tables),
                [pltpu.VMEM((BLOCK + EXTRA, y_blocks * BLOCK), BF16)])
    got = exchange(sent, "space")
    packed = (2 * rows // half, columns // 2)
    inputs = (members, weight)
    near, arrived = landing(inputs)
    terms = call(functools.partial(row_kernel, x_blocks), (half,) + packed,
                 (got,) + inputs + tuple(x_tables),
                 near + [pltpu.VMEM((rows, columns), BF16), arrived],
                 [pltpu.VMEM, pltpu.HBM, pltpu.HBM])
    part = call(sum_kernel, (1,) + packed, (exchange(terms, "mem", halves),))
    other = lax.ppermute(part, "mem", twins)
    result = call(functools.partial(add_kernel, float(mem - 1)), (half,) + packed, (part, other))
    return call(final_kernel, (1, rows, columns), (mask, exchange(result, "mem", halves)))


def solution(mesh):
    placed = (
        P(None, "space", None),
        P(None, "space", None),
        P("mem", None, "space", None),
        P("space", None),
        P(),
        P(),
        P(),
        P(),
    )
    return jax.shard_map(
        local, mesh=mesh, in_specs=placed, out_specs=P(None, "space", None), check_vma=False
    )
```

```python
import functools

import jax
import jax.numpy as jnp
from jax import lax
from jax.experimental import pallas as pl
from jax.experimental.pallas import tpu as pltpu
from jax.sharding import PartitionSpec as P


BLOCK = 128
LAST = BLOCK - 1
NSTEP = 7
HALF = 64
EXTRA = 16
FOLD = EXTRA // 2
F32 = jnp.float32
BF16 = jnp.bfloat16
GROUP = BLOCK // (2 * NSTEP)
VMEM_LIMIT = 16 * 2**20
WIDE_LIMIT = 60 * 2**20


def dot(a, b):
    return lax.dot_general(a, b, (((1,), (0,)), ((), ())), preferred_element_type=F32)


def dot_nt(a, b):
    return lax.dot_general(a, b, (((1,), (1,)), ((), ())), preferred_element_type=F32)


def round_up(value, unit):
    return (value + unit - 1) // unit * unit


def groups_of(nb):
    return (nb + GROUP - 1) // GROUP


def place(j):
    return j // GROUP * BLOCK + j % GROUP * 2 * NSTEP


def prepare_kernel(nb, c_ref, g_ref, pow_ref, map_a_ref, map_f_ref, rows_ref, columns_ref, turned_ref,
                   edges, rows, columns, rmat, qmat, ct, high2, low2, high3, low3, high4, low4,
                   few_rows, few_columns):
    pad = round_up(nb, 8)
    kp = map_a_ref.shape[0]
    lane = lax.broadcasted_iota(jnp.int32, (16, BLOCK), 1)
    row = lax.broadcasted_iota(jnp.int32, (16, BLOCK), 0)
    select = jnp.where((row < 2) & (lane == row * LAST), 1.0, 0.0)
    edges[...] = jnp.zeros_like(edges)
    rows[...] = jnp.zeros_like(rows)
    columns[...] = jnp.zeros_like(columns)

    def stack(first, *pairs):
        out = first
        for at, (top, bottom) in enumerate(pairs):
            out = jnp.where(row == 2 * at + 2, top, jnp.where(row == 2 * at + 3, bottom, out))
        return out.astype(BF16)

    def split(full):
        high = full.astype(BF16)
        return high, (full - high.astype(F32)).astype(BF16)

    def put_row(j, k, top, bottom):
        at = place(j) + 2 * k - 2
        rows[at:at + 1, :] = bottom
        rows[at + 1:at + 2, :] = top
        edges[k - 1, 0, j:j + 1, :] = top
        edges[k - 1, 1, j:j + 1, :] = bottom

    def put_column(j, k, left, right):
        at = place(j) + 2 * k - 2
        columns[at:at + 1, :] = right
        columns[at + 1:at + 2, :] = left

    def ends(full):
        return full[0:1], full[LAST:BLOCK]

    def pair(rows, first):
        return rows[first:first + 1], rows[first + 1:first + 2]

    for j in range(nb):
        g = g_ref[j]
        g_full = g.astype(F32)
        second = dot(g, g)
        high2[j], low2[j] = split(second)
        put_row(j, 1, *ends(g_full))
        put_row(j, 2, *ends(second))
        few_rows[j] = stack(jnp.zeros((16, BLOCK), F32), ends(g_full), ends(second))
        found = dot_nt(select.astype(BF16), g)
        put_column(j, 1, *pair(found, 0))
        few_columns[j] = stack(select, pair(found, 0)).astype(F32)

    for j in range(nb):
        both = jnp.concatenate([g_ref[j], high2[j]], axis=0)
        result = dot(jnp.concatenate([both, both], axis=1), jnp.concatenate([high2[j], low2[j]], axis=0))
        third, fourth = result[0:BLOCK], result[BLOCK:2 * BLOCK] + dot(low2[j], high2[j])
        high3[j], low3[j] = split(third)
        high4[j], low4[j] = split(fourth)
        put_row(j, 3, *ends(third))
        put_row(j, 4, *ends(fourth))
        old = few_columns[j]
        found = dot_nt(old.astype(BF16), high2[j])
        put_column(j, 2, *pair(found, 0))
        put_column(j, 3, *pair(found, 2))
        few_columns[j] = stack(old, pair(old, 2), pair(found, 0), pair(found, 2)).astype(F32)

    for j in range(nb):
        left = jnp.concatenate([high3[j], few_rows[j]], axis=0)
        result = dot(jnp.concatenate([left, left], axis=1), jnp.concatenate([high4[j], low4[j]], axis=0))
        seventh = result[0:BLOCK] + dot(low3[j], high4[j])
        pow_ref[j] = seventh.astype(BF16)
        put_row(j, 5, *pair(result, BLOCK + 2))
        put_row(j, 6, *pair(result, BLOCK + 4))
        put_row(j, 7, *ends(seventh))
        found = dot_nt(few_columns[j].astype(BF16), high4[j])
        for k in range(4):
            put_column(j, 4 + k, *pair(found, 2 * k))

    rows_ref[...] = rows[...].astype(BF16)
    columns_ref[...] = columns[...].astype(BF16)
    for group in range(groups_of(nb)):
        turned_ref[group] = columns[group * BLOCK:(group + 1) * BLOCK, :].T.astype(BF16)

    def corner(run, k, a, b):
        if run == 1:
            a, b = b, a
        return edges[k - 1, a, :, 0:1] if b == 0 else edges[k - 1, a, :, LAST:BLOCK]

    unit = lax.broadcasted_iota(jnp.int32, (1, BLOCK), 1)
    runs = range(2)
    gain_s = [jnp.broadcast_to(corner(run, 1, 0, 1), (pad, BLOCK)) for run in runs]
    gain_t = [jnp.broadcast_to(corner(run, 1, 1, 0), (pad, BLOCK)) for run in runs]
    gain_0 = jnp.broadcast_to(corner(0, 1, 0, 0), (pad, BLOCK))
    rmat[...] = jnp.zeros_like(rmat)
    qmat[...] = jnp.zeros_like(qmat)
    ct[...] = jnp.zeros_like(ct)
    s_row = [jnp.zeros((1, BLOCK), F32) for run in runs]
    p_rows = [[], []]
    for j in range(nb):
        for run in runs:
            p_rows[run].append(jnp.where(unit == pad + j, 1.0, 0.0) + gain_0[j:j + 1] * s_row[run])
            if j + 1 < nb:
                s_row[run] = c_ref[j] * (jnp.where(unit == j, 1.0, 0.0) + gain_s[run][j:j + 1] * s_row[run])
                rmat[run, j + 1:j + 2, :] = s_row[run]
    t_row = [jnp.zeros((1, BLOCK), F32) for run in runs]
    for j in range(nb - 2, -1, -1):
        for run in runs:
            t_row[run] = c_ref[j] * (p_rows[run][j + 1] + gain_t[run][j + 1:j + 2] * t_row[run])
            rmat[run, pad + j:pad + j + 1, :] = t_row[run]

    block = lax.broadcasted_iota(jnp.int32, (pad, kp), 0)
    first = block * (2 * NSTEP)
    for group in range(1, groups_of(nb)):
        first += jnp.where(block >= group * GROUP, BLOCK - GROUP * 2 * NSTEP, 0)
    first = lax.broadcasted_iota(jnp.int32, (pad, kp), 1) - first
    sources, trailing = [[], []], [[], []]
    for k in range(NSTEP):
        for run in runs:
            q_last = jnp.where((block < nb) & (first == 2 * k), 1.0, 0.0)
            q_first = jnp.where((block < nb) & (first == 2 * k + 1), 1.0, 0.0)
            for m in range(k):
                s_old, t_old = sources[run][m], trailing[run][m]
                q_last += corner(run, k - m + 1, 0, 1) * s_old + corner(run, k - m + 1, 1, 1) * t_old
                q_first += corner(run, k - m + 1, 0, 0) * s_old + corner(run, k - m + 1, 1, 0) * t_old
            qmat[run, 0:pad, :] = q_last
            qmat[run, pad:2 * pad, :] = q_first
        for run in runs:
            now = lax.dot_general(rmat[run], qmat[run], (((1,), (0,)), ((), ())),
                                  precision=lax.Precision.HIGHEST, preferred_element_type=F32)
            sources[run].append(now[0:pad])
            trailing[run].append(now[pad:2 * pad])
            for j in range(nb):
                at = place(j) + (NSTEP - 1 - k) * 2
                ct[run, at:at + 1, :] = now[pad + j:pad + j + 1]
                ct[run, at + 1:at + 2, :] = now[j:j + 1]
    map_a_ref[...] = ct[0].astype(BF16)
    map_f_ref[...] = ct[1].astype(BF16)


def prepare(inverse, coupling):
    nb = inverse.shape[0]
    kp, pad = groups_of(nb) * BLOCK, round_up(nb, 8)
    vmem = pl.BlockSpec(memory_space=pltpu.VMEM)
    shapes = [(nb, BLOCK, BLOCK), (kp, kp), (kp, kp), (kp, BLOCK), (kp, BLOCK), (groups_of(nb), BLOCK, BLOCK)]
    return pl.pallas_call(
        functools.partial(prepare_kernel, nb),
        out_shape=tuple(jax.ShapeDtypeStruct(shape, BF16) for shape in shapes),
        in_specs=[pl.BlockSpec(memory_space=pltpu.SMEM), vmem],
        out_specs=(vmem,) * len(shapes),
        scratch_shapes=[
            pltpu.VMEM((NSTEP, 2, pad, BLOCK), F32),
            pltpu.VMEM((kp, BLOCK), F32),
            pltpu.VMEM((kp, BLOCK), F32),
            pltpu.VMEM((2, 2 * pad, BLOCK), F32),
            pltpu.VMEM((2, BLOCK, kp), F32),
            pltpu.VMEM((2, kp, kp), F32),
        ] + [pltpu.VMEM((nb, BLOCK, BLOCK), BF16)] * 6 + [
            pltpu.VMEM((nb, 16, BLOCK), BF16),
            pltpu.VMEM((nb, 16, BLOCK), F32),
        ],
        compiler_params=pltpu.CompilerParams(vmem_limit_bytes=VMEM_LIMIT),
        cost_estimate=pl.CostEstimate(
            flops=nb * 400 * BLOCK**3, bytes_accessed=4000000, transcendentals=0),
    )(coupling, inverse)


def run_steps(lines, nb, pow_ref, map_ref, in_ref, out_ref, adjoint):
    count = lines.shape[0]
    lane = lax.broadcasted_iota(jnp.int32, (count, BLOCK), 1)
    owned = [(lane >= at * 2 * NSTEP) & (lane < (at + 1) * 2 * NSTEP) for at in range(min(nb, GROUP))]
    blocks = [slice(j * BLOCK, (j + 1) * BLOCK) for j in range(nb)]
    products = []
    for group in range(groups_of(nb)):
        edge = in_ref[group * BLOCK:(group + 1) * BLOCK, :]
        kept = jnp.zeros((count, BLOCK), F32)
        mine = range(group * GROUP, min(nb, (group + 1) * GROUP))
        if count < BLOCK:
            stacked = dot_nt(jnp.concatenate([lines[:, blocks[j]] for j in mine], axis=0), edge)
            found = [stacked[at * count:(at + 1) * count] for at in range(len(mine))]
        else:
            found = [dot_nt(lines[:, blocks[j]], edge) for j in mine]
        for at in range(len(mine)):
            kept = jnp.where(owned[at], found[at], kept)
        products.append(kept.astype(BF16))
    coupled = dot_nt(jnp.concatenate(products, axis=1), map_ref[...])
    results = []
    for j in range(nb):
        group = j // GROUP
        mine = jnp.where(owned[j % GROUP], coupled[:, group * BLOCK:(group + 1) * BLOCK], 0.0).astype(BF16)
        left = jnp.concatenate([lines[:, blocks[j]], mine], axis=1)
        if adjoint:
            edge = out_ref[group * BLOCK:(group + 1) * BLOCK, :]
            results.append(dot(left, jnp.concatenate([pow_ref[j], edge], axis=0)))
        else:
            results.append(dot_nt(left, jnp.concatenate([pow_ref[j], out_ref[group]], axis=1)))
    return results


def run_both(lines, nb, pow_ref, map_a_ref, map_f_ref, rows_ref, columns_ref, turned_ref):
    for j, block in enumerate(run_steps(lines, nb, pow_ref, map_a_ref, columns_ref, rows_ref, True)):
        lines[:, j * BLOCK:(j + 1) * BLOCK] = block.astype(BF16)
    return run_steps(lines, nb, pow_ref, map_f_ref, rows_ref, turned_ref, False)


def beside(left, right):
    return jnp.where(lax.broadcasted_iota(jnp.int32, left.shape, 1) < HALF, left, right)


def swap(tile):
    return pltpu.roll(tile, HALF, 1)


def start_kernel(increment_hbm, mask_hbm, members_hbm, weight_hbm, out_ref,
                 increment_ref, mask_ref, members_ref, weight_ref, arrived):
    copies = [
        pltpu.make_async_copy(source, target, arrived.at[at])
        for at, (source, target) in enumerate((
            (increment_hbm, increment_ref), (mask_hbm, mask_ref),
            (members_hbm, members_ref), (weight_hbm, weight_ref)))
    ]
    for copy in copies:
        copy.start()
    for copy in copies:
        copy.wait()
    shares = out_ref.shape[0]

    def values(at):
        return (weight_ref[:, at] * mask_ref[0, :, at].astype(F32) * members_ref[0, 0, :, at].astype(F32)
                * increment_ref[0, :, at].astype(F32))

    for half in range(2):
        tail = values(slice((shares + half) * BLOCK, (shares + half + 1) * BLOCK))
        turned = jnp.concatenate([tail, tail], axis=0).T
        for s in range(8):
            out_ref[half * 8 + s, HALF:HALF + FOLD, :] = beside(
                turned[s * EXTRA:s * EXTRA + FOLD], turned[s * EXTRA + FOLD:(s + 1) * EXTRA]).astype(BF16)
    for s in range(shares):
        out_ref[s, 0:HALF, :] = values(slice(s * BLOCK, (s + 1) * BLOCK)).astype(BF16)


def column_kernel(nb, in_ref, *refs):
    *tables, out_ref, lines = refs
    for j in range(nb):
        at = slice(j * BLOCK, (j + 1) * BLOCK)
        square = jnp.concatenate([in_ref[2 * j, 0:HALF, :], in_ref[2 * j + 1, 0:HALF, :]], axis=0)
        lines[0:BLOCK, at] = square.astype(F32).T.astype(BF16)
        even = in_ref[2 * j, HALF:HALF + FOLD, :].astype(F32)
        odd = in_ref[2 * j + 1, HALF:HALF + FOLD, :].astype(F32)
        tail = jnp.concatenate([beside(even, swap(odd)), beside(swap(even), odd)], axis=0)
        lines[BLOCK:BLOCK + EXTRA, at] = tail.astype(BF16)
    for j, block in enumerate(run_both(lines, nb, *tables)):
        square = block[0:BLOCK].T.astype(BF16)
        top, bottom = block[BLOCK:BLOCK + FOLD], block[BLOCK + FOLD:BLOCK + EXTRA]
        tails = beside(top, swap(bottom)), beside(swap(top), bottom)
        for half in range(2):
            out_ref[2 * j + half, 0:HALF, :] = square[half * HALF:(half + 1) * HALF]
            out_ref[2 * j + half, HALF:HALF + FOLD, :] = tails[half].astype(BF16)


def row_kernel(nb, in_ref, *refs):
    members_hbm, weight_hbm, *tables, out_ref, members_ref, weight_ref, lines, arrived = refs
    copies = [pltpu.make_async_copy(members_hbm, members_ref, arrived.at[0]),
              pltpu.make_async_copy(weight_hbm, weight_ref, arrived.at[1])]
    for copy in copies:
        copy.start()
    shares = in_ref.shape[0]
    for s in range(shares):
        lines[:, s * BLOCK:(s + 1) * BLOCK] = in_ref[s, 0:HALF, :]
    for half in range(2):
        folded = [in_ref[half * 8 + s, HALF:HALF + FOLD, :].astype(F32) for s in range(8)]
        tail = jnp.concatenate([part for tile in folded for part in (tile, swap(tile))], axis=0).T[0:HALF]
        at = (shares + half) * BLOCK
        lines[:, at:at + BLOCK] = tail.astype(BF16)
    blocks = run_both(lines, nb, *tables)
    for copy in copies:
        copy.wait()
    for j in range(nb):
        at = slice(j * BLOCK, (j + 1) * BLOCK)
        term = members_ref[0, 0, :, at].astype(F32) * weight_ref[:, at] * blocks[j]
        for taker in range(out_ref.shape[0]):
            out_ref[taker, :, at] = term[taker * 8:taker * 8 + 8].astype(BF16)


def sum_kernel(in_ref, out_ref):
    total = in_ref[0].astype(F32)
    for source in range(1, in_ref.shape[0]):
        total += in_ref[source].astype(F32)
    out_ref[0] = total.astype(BF16)


def add_kernel(one_ref, two_ref, out_ref):
    out_ref[0] = (one_ref[0].astype(F32) + two_ref[0].astype(F32)).astype(BF16)


def final_kernel(scale, own_ref, one_ref, two_ref, mask_ref, out_ref):
    rows = out_ref.shape[1]
    mask = mask_ref[0, pl.ds(pl.multiple_of(own_ref[0] * rows, rows), rows), :].astype(F32)
    total = (mask * (one_ref[0].astype(F32) + two_ref[0].astype(F32)) / scale).astype(BF16)
    for target in range(out_ref.shape[0]):
        out_ref[target] = total


def call(kernel, out_shape, operands, scratch=(), spaces=(), limit=VMEM_LIMIT):
    spaces = tuple(spaces) + (pltpu.VMEM,) * (len(operands) - len(spaces))
    return pl.pallas_call(
        kernel,
        out_shape=jax.ShapeDtypeStruct(out_shape, BF16),
        in_specs=[pl.BlockSpec(memory_space=space) for space in spaces],
        out_specs=pl.BlockSpec(memory_space=pltpu.VMEM),
        scratch_shapes=list(scratch),
        compiler_params=pltpu.CompilerParams(vmem_limit_bytes=limit),
        cost_estimate=pl.CostEstimate(flops=1000000, bytes_accessed=2000000, transcendentals=0),
    )(*operands)


def landing(arrays):
    return [pltpu.VMEM(array.shape, array.dtype) for array in arrays], pltpu.SemaphoreType.DMA((len(arrays),))


def exchange(array, axis, groups=None):
    return lax.all_to_all(array, axis, split_axis=0, concat_axis=0, tiled=True, axis_index_groups=groups)


def local(increment, mask, members, weight, x_inverse, x_coupling, y_inverse, y_coupling):
    _, _, rows, columns = members.shape
    space, mem = lax.axis_size("space"), lax.axis_size("mem")
    x_blocks, y_blocks = x_inverse.shape[0], y_inverse.shape[0]
    close = 8
    apart = mem // close
    near_groups = [[z * close + i for i in range(close)] for z in range(apart)]
    far_groups = [[z * close + i for z in range(apart)] for i in range(close)]
    share = (HALF + FOLD, BLOCK)

    y_tables = prepare(y_inverse, y_coupling)
    x_tables = prepare(x_inverse, x_coupling)

    inputs = (increment, mask, members, weight)
    near, arrived = landing(inputs)
    sent = call(start_kernel, (space,) + share, inputs,
                near + [arrived], [pltpu.HBM] * 4, WIDE_LIMIT)
    got, x_tables, y_tables = lax.optimization_barrier((exchange(sent, "space"), x_tables, y_tables))
    sent = call(functools.partial(column_kernel, y_blocks), (space,) + share, (got,) + tuple(y_tables),
                [pltpu.VMEM((BLOCK + EXTRA, y_blocks * BLOCK), BF16)])
    got = exchange(sent, "space")
    own = (lax.axis_index("mem") % close).astype(jnp.int32)[None]
    packed = (rows // close, columns)
    inputs = (members, weight)
    near, arrived = landing(inputs)
    terms = call(functools.partial(row_kernel, x_blocks), (close,) + packed,
                 (got,) + inputs + tuple(x_tables),
                 near + [pltpu.VMEM((rows, columns), BF16), arrived],
                 [pltpu.VMEM, pltpu.HBM, pltpu.HBM])
    terms = exchange(terms, "mem", near_groups)
    part = call(sum_kernel, (1,) + packed, (terms,))
    for step in range(2):
        pairs = []
        for device in range(mem):
            z, odd = device // close, (device + step) % 2
            pairs.append((device, ((z ^ 1) if odd == 0 else ((z - 1) ^ 1) + 1) % apart * close + device % close))
        other = lax.ppermute(part, "mem", pairs)
        if step == 0:
            part = call(add_kernel, (1,) + packed, (part, other))
    result = call(functools.partial(final_kernel, float(mem - 1)), (close,) + packed, (own, part, other, mask),
                  spaces=[pltpu.SMEM])
    return exchange(result, "mem", near_groups).reshape(1, rows, columns)


def solution(mesh):
    placed = (
        P(None, "space", None),
        P(None, "space", None),
        P("mem", None, "space", None),
        P("space", None),
        P(),
        P(),
        P(),
        P(),
    )
    return jax.shard_map(
        local, mesh=mesh, in_specs=placed, out_specs=P(None, "space", None), check_vma=False
    )
```

```python
import functools

import jax
import jax.numpy as jnp
from jax import lax
from jax.experimental import pallas as pl
from jax.experimental.pallas import tpu as pltpu
from jax.sharding import PartitionSpec as P


BLOCK = 128
LAST = BLOCK - 1
NSTEP = 7
HALF = 64
EXTRA = 16
FOLD = EXTRA // 2
F32 = jnp.float32
BF16 = jnp.bfloat16
GROUP = BLOCK // (2 * NSTEP)
VMEM_LIMIT = 16 * 2**20
WIDE_LIMIT = 60 * 2**20


def dot(a, b):
    return lax.dot_general(a, b, (((1,), (0,)), ((), ())), preferred_element_type=F32)


def dot_nt(a, b):
    return lax.dot_general(a, b, (((1,), (1,)), ((), ())), preferred_element_type=F32)


def round_up(value, unit):
    return (value + unit - 1) // unit * unit


def groups_of(nb):
    return (nb + GROUP - 1) // GROUP


def place(j):
    return j // GROUP * BLOCK + j % GROUP * 2 * NSTEP


def prepare_kernel(nb, c_ref, g_ref, pow_ref, map_a_ref, map_f_ref, rows_ref, columns_ref, turned_ref,
                   edges, rows, columns, rmat, qmat, ct, high2, low2, high3, low3, high4, low4,
                   few_rows, few_columns):
    pad = round_up(nb, 8)
    kp = map_a_ref.shape[0]
    lane = lax.broadcasted_iota(jnp.int32, (16, BLOCK), 1)
    row = lax.broadcasted_iota(jnp.int32, (16, BLOCK), 0)
    select = jnp.where((row < 2) & (lane == row * LAST), 1.0, 0.0)
    edges[...] = jnp.zeros_like(edges)
    rows[...] = jnp.zeros_like(rows)
    columns[...] = jnp.zeros_like(columns)

    def stack(first, *pairs):
        out = first
        for at, (top, bottom) in enumerate(pairs):
            out = jnp.where(row == 2 * at + 2, top, jnp.where(row == 2 * at + 3, bottom, out))
        return out.astype(BF16)

    def split(full):
        high = full.astype(BF16)
        return high, (full - high.astype(F32)).astype(BF16)

    def put_row(j, k, top, bottom):
        at = place(j) + 2 * k - 2
        rows[at:at + 1, :] = bottom
        rows[at + 1:at + 2, :] = top
        edges[k - 1, 0, j:j + 1, :] = top
        edges[k - 1, 1, j:j + 1, :] = bottom

    def put_column(j, k, left, right):
        at = place(j) + 2 * k - 2
        columns[at:at + 1, :] = right
        columns[at + 1:at + 2, :] = left

    def ends(full):
        return full[0:1], full[LAST:BLOCK]

    def pair(rows, first):
        return rows[first:first + 1], rows[first + 1:first + 2]

    for j in range(nb):
        g = g_ref[j]
        g_full = g.astype(F32)
        second = dot(g, g)
        high2[j], low2[j] = split(second)
        put_row(j, 1, *ends(g_full))
        put_row(j, 2, *ends(second))
        few_rows[j] = stack(jnp.zeros((16, BLOCK), F32), ends(g_full), ends(second))
        found = dot_nt(select.astype(BF16), g)
        put_column(j, 1, *pair(found, 0))
        few_columns[j] = stack(select, pair(found, 0)).astype(F32)

    for j in range(nb):
        both = jnp.concatenate([g_ref[j], high2[j]], axis=0)
        result = dot(jnp.concatenate([both, both], axis=1), jnp.concatenate([high2[j], low2[j]], axis=0))
        third, fourth = result[0:BLOCK], result[BLOCK:2 * BLOCK] + dot(low2[j], high2[j])
        high3[j], low3[j] = split(third)
        high4[j], low4[j] = split(fourth)
        put_row(j, 3, *ends(third))
        put_row(j, 4, *ends(fourth))
        old = few_columns[j]
        found = dot_nt(old.astype(BF16), high2[j])
        put_column(j, 2, *pair(found, 0))
        put_column(j, 3, *pair(found, 2))
        few_columns[j] = stack(old, pair(old, 2), pair(found, 0), pair(found, 2)).astype(F32)

    for j in range(nb):
        left = jnp.concatenate([high3[j], few_rows[j]], axis=0)
        result = dot(jnp.concatenate([left, left], axis=1), jnp.concatenate([high4[j], low4[j]], axis=0))
        seventh = result[0:BLOCK] + dot(low3[j], high4[j])
        pow_ref[j] = seventh.astype(BF16)
        put_row(j, 5, *pair(result, BLOCK + 2))
        put_row(j, 6, *pair(result, BLOCK + 4))
        put_row(j, 7, *ends(seventh))
        found = dot_nt(few_columns[j].astype(BF16), high4[j])
        for k in range(4):
            put_column(j, 4 + k, *pair(found, 2 * k))

    rows_ref[...] = rows[...].astype(BF16)
    columns_ref[...] = columns[...].astype(BF16)
    for group in range(groups_of(nb)):
        turned_ref[group] = columns[group * BLOCK:(group + 1) * BLOCK, :].T.astype(BF16)

    def corner(run, k, a, b):
        if run == 1:
            a, b = b, a
        return edges[k - 1, a, :, 0:1] if b == 0 else edges[k - 1, a, :, LAST:BLOCK]

    unit = lax.broadcasted_iota(jnp.int32, (1, BLOCK), 1)
    runs = range(2)
    gain_s = [jnp.broadcast_to(corner(run, 1, 0, 1), (pad, BLOCK)) for run in runs]
    gain_t = [jnp.broadcast_to(corner(run, 1, 1, 0), (pad, BLOCK)) for run in runs]
    gain_0 = jnp.broadcast_to(corner(0, 1, 0, 0), (pad, BLOCK))
    rmat[...] = jnp.zeros_like(rmat)
    qmat[...] = jnp.zeros_like(qmat)
    ct[...] = jnp.zeros_like(ct)
    s_row = [jnp.zeros((1, BLOCK), F32) for run in runs]
    p_rows = [[], []]
    for j in range(nb):
        for run in runs:
            p_rows[run].append(jnp.where(unit == pad + j, 1.0, 0.0) + gain_0[j:j + 1] * s_row[run])
            if j + 1 < nb:
                s_row[run] = c_ref[j] * (jnp.where(unit == j, 1.0, 0.0) + gain_s[run][j:j + 1] * s_row[run])
                rmat[run, j + 1:j + 2, :] = s_row[run]
    t_row = [jnp.zeros((1, BLOCK), F32) for run in runs]
    for j in range(nb - 2, -1, -1):
        for run in runs:
            t_row[run] = c_ref[j] * (p_rows[run][j + 1] + gain_t[run][j + 1:j + 2] * t_row[run])
            rmat[run, pad + j:pad + j + 1, :] = t_row[run]

    block = lax.broadcasted_iota(jnp.int32, (pad, kp), 0)
    first = block * (2 * NSTEP)
    for group in range(1, groups_of(nb)):
        first += jnp.where(block >= group * GROUP, BLOCK - GROUP * 2 * NSTEP, 0)
    first = lax.broadcasted_iota(jnp.int32, (pad, kp), 1) - first
    sources, trailing = [[], []], [[], []]
    for k in range(NSTEP):
        for run in runs:
            q_last = jnp.where((block < nb) & (first == 2 * k), 1.0, 0.0)
            q_first = jnp.where((block < nb) & (first == 2 * k + 1), 1.0, 0.0)
            for m in range(k):
                s_old, t_old = sources[run][m], trailing[run][m]
                q_last += corner(run, k - m + 1, 0, 1) * s_old + corner(run, k - m + 1, 1, 1) * t_old
                q_first += corner(run, k - m + 1, 0, 0) * s_old + corner(run, k - m + 1, 1, 0) * t_old
            qmat[run, 0:pad, :] = q_last
            qmat[run, pad:2 * pad, :] = q_first
        for run in runs:
            now = lax.dot_general(rmat[run], qmat[run], (((1,), (0,)), ((), ())),
                                  precision=lax.Precision.HIGHEST, preferred_element_type=F32)
            sources[run].append(now[0:pad])
            trailing[run].append(now[pad:2 * pad])
            for j in range(nb):
                at = place(j) + (NSTEP - 1 - k) * 2
                ct[run, at:at + 1, :] = now[pad + j:pad + j + 1]
                ct[run, at + 1:at + 2, :] = now[j:j + 1]
    map_a_ref[...] = ct[0].astype(BF16)
    map_f_ref[...] = ct[1].astype(BF16)


def prepare(inverse, coupling):
    nb = inverse.shape[0]
    kp, pad = groups_of(nb) * BLOCK, round_up(nb, 8)
    vmem = pl.BlockSpec(memory_space=pltpu.VMEM)
    shapes = [(nb, BLOCK, BLOCK), (kp, kp), (kp, kp), (kp, BLOCK), (kp, BLOCK), (groups_of(nb), BLOCK, BLOCK)]
    return pl.pallas_call(
        functools.partial(prepare_kernel, nb),
        out_shape=tuple(jax.ShapeDtypeStruct(shape, BF16) for shape in shapes),
        in_specs=[pl.BlockSpec(memory_space=pltpu.SMEM), vmem],
        out_specs=(vmem,) * len(shapes),
        scratch_shapes=[
            pltpu.VMEM((NSTEP, 2, pad, BLOCK), F32),
            pltpu.VMEM((kp, BLOCK), F32),
            pltpu.VMEM((kp, BLOCK), F32),
            pltpu.VMEM((2, 2 * pad, BLOCK), F32),
            pltpu.VMEM((2, BLOCK, kp), F32),
            pltpu.VMEM((2, kp, kp), F32),
        ] + [pltpu.VMEM((nb, BLOCK, BLOCK), BF16)] * 6 + [
            pltpu.VMEM((nb, 16, BLOCK), BF16),
            pltpu.VMEM((nb, 16, BLOCK), F32),
        ],
        compiler_params=pltpu.CompilerParams(vmem_limit_bytes=VMEM_LIMIT),
        cost_estimate=pl.CostEstimate(
            flops=nb * 400 * BLOCK**3, bytes_accessed=4000000, transcendentals=0),
    )(coupling, inverse)


def run_steps(lines, nb, pow_ref, map_ref, in_ref, out_ref, adjoint):
    count = lines.shape[0]
    lane = lax.broadcasted_iota(jnp.int32, (count, BLOCK), 1)
    owned = [(lane >= at * 2 * NSTEP) & (lane < (at + 1) * 2 * NSTEP) for at in range(min(nb, GROUP))]
    blocks = [slice(j * BLOCK, (j + 1) * BLOCK) for j in range(nb)]
    products = []
    for group in range(groups_of(nb)):
        edge = in_ref[group * BLOCK:(group + 1) * BLOCK, :]
        kept = jnp.zeros((count, BLOCK), F32)
        mine = range(group * GROUP, min(nb, (group + 1) * GROUP))
        if count < BLOCK:
            stacked = dot_nt(jnp.concatenate([lines[:, blocks[j]] for j in mine], axis=0), edge)
            found = [stacked[at * count:(at + 1) * count] for at in range(len(mine))]
        else:
            found = [dot_nt(lines[:, blocks[j]], edge) for j in mine]
        for at in range(len(mine)):
            kept = jnp.where(owned[at], found[at], kept)
        products.append(kept.astype(BF16))
    coupled = dot_nt(jnp.concatenate(products, axis=1), map_ref[...])
    results = []
    for j in range(nb):
        group = j // GROUP
        mine = jnp.where(owned[j % GROUP], coupled[:, group * BLOCK:(group + 1) * BLOCK], 0.0).astype(BF16)
        left = jnp.concatenate([lines[:, blocks[j]], mine], axis=1)
        if adjoint:
            edge = out_ref[group * BLOCK:(group + 1) * BLOCK, :]
            results.append(dot(left, jnp.concatenate([pow_ref[j], edge], axis=0)))
        else:
            results.append(dot_nt(left, jnp.concatenate([pow_ref[j], out_ref[group]], axis=1)))
    return results


def run_both(lines, nb, pow_ref, map_a_ref, map_f_ref, rows_ref, columns_ref, turned_ref):
    for j, block in enumerate(run_steps(lines, nb, pow_ref, map_a_ref, columns_ref, rows_ref, True)):
        lines[:, j * BLOCK:(j + 1) * BLOCK] = block.astype(BF16)
    return run_steps(lines, nb, pow_ref, map_f_ref, rows_ref, turned_ref, False)


def beside(left, right):
    return jnp.where(lax.broadcasted_iota(jnp.int32, left.shape, 1) < HALF, left, right)


def swap(tile):
    return pltpu.roll(tile, HALF, 1)


def start_kernel(increment_hbm, mask_hbm, members_hbm, weight_hbm, out_ref,
                 increment_ref, mask_ref, members_ref, weight_ref, arrived):
    copies = [
        pltpu.make_async_copy(source, target, arrived.at[at])
        for at, (source, target) in enumerate((
            (increment_hbm, increment_ref), (mask_hbm, mask_ref),
            (members_hbm, members_ref), (weight_hbm, weight_ref)))
    ]
    for copy in copies:
        copy.start()
    for copy in copies:
        copy.wait()
    shares = out_ref.shape[0]

    def values(at):
        return (weight_ref[:, at] * mask_ref[0, :, at].astype(F32) * members_ref[0, 0, :, at].astype(F32)
                * increment_ref[0, :, at].astype(F32))

    for half in range(2):
        tail = values(slice((shares + half) * BLOCK, (shares + half + 1) * BLOCK))
        turned = jnp.concatenate([tail, tail], axis=0).T
        for s in range(8):
            out_ref[half * 8 + s, HALF:HALF + FOLD, :] = beside(
                turned[s * EXTRA:s * EXTRA + FOLD], turned[s * EXTRA + FOLD:(s + 1) * EXTRA]).astype(BF16)
    for s in range(shares):
        out_ref[s, 0:HALF, :] = values(slice(s * BLOCK, (s + 1) * BLOCK)).astype(BF16)


def column_kernel(nb, in_ref, *refs):
    *tables, out_ref, lines = refs
    for j in range(nb):
        at = slice(j * BLOCK, (j + 1) * BLOCK)
        square = jnp.concatenate([in_ref[2 * j, 0:HALF, :], in_ref[2 * j + 1, 0:HALF, :]], axis=0)
        lines[0:BLOCK, at] = square.astype(F32).T.astype(BF16)
        even = in_ref[2 * j, HALF:HALF + FOLD, :].astype(F32)
        odd = in_ref[2 * j + 1, HALF:HALF + FOLD, :].astype(F32)
        tail = jnp.concatenate([beside(even, swap(odd)), beside(swap(even), odd)], axis=0)
        lines[BLOCK:BLOCK + EXTRA, at] = tail.astype(BF16)
    for j, block in enumerate(run_both(lines, nb, *tables)):
        square = block[0:BLOCK].T.astype(BF16)
        top, bottom = block[BLOCK:BLOCK + FOLD], block[BLOCK + FOLD:BLOCK + EXTRA]
        tails = beside(top, swap(bottom)), beside(swap(top), bottom)
        for half in range(2):
            out_ref[2 * j + half, 0:HALF, :] = square[half * HALF:(half + 1) * HALF]
            out_ref[2 * j + half, HALF:HALF + FOLD, :] = tails[half].astype(BF16)


def row_kernel(nb, in_ref, *refs):
    members_hbm, weight_hbm, *tables, out_ref, members_ref, weight_ref, lines, arrived = refs
    copies = [pltpu.make_async_copy(members_hbm, members_ref, arrived.at[0]),
              pltpu.make_async_copy(weight_hbm, weight_ref, arrived.at[1])]
    for copy in copies:
        copy.start()
    shares = in_ref.shape[0]
    for s in range(shares):
        lines[:, s * BLOCK:(s + 1) * BLOCK] = in_ref[s, 0:HALF, :]
    for half in range(2):
        folded = [in_ref[half * 8 + s, HALF:HALF + FOLD, :].astype(F32) for s in range(8)]
        tail = jnp.concatenate([part for tile in folded for part in (tile, swap(tile))], axis=0).T[0:HALF]
        at = (shares + half) * BLOCK
        lines[:, at:at + BLOCK] = tail.astype(BF16)
    blocks = run_both(lines, nb, *tables)
    for copy in copies:
        copy.wait()
    for j in range(nb):
        at = slice(j * BLOCK, (j + 1) * BLOCK)
        term = members_ref[0, 0, :, at].astype(F32) * weight_ref[:, at] * blocks[j]
        for taker in range(out_ref.shape[0]):
            out_ref[taker, :, at] = term[taker * 8:taker * 8 + 8].astype(BF16)


def sum_kernel(in_ref, out_ref):
    total = in_ref[0].astype(F32)
    for source in range(1, in_ref.shape[0]):
        total += in_ref[source].astype(F32)
    out_ref[0] = total.astype(BF16)


def add_kernel(one_ref, two_ref, out_ref):
    out_ref[0] = (one_ref[0].astype(F32) + two_ref[0].astype(F32)).astype(BF16)


def final_kernel(scale, own_ref, one_ref, two_ref, mask_ref, out_ref):
    rows = out_ref.shape[1]
    mask = mask_ref[0, pl.ds(pl.multiple_of(own_ref[0] * rows, rows), rows), :].astype(F32)
    total = (mask * (one_ref[0].astype(F32) + two_ref[0].astype(F32)) / scale).astype(BF16)
    for target in range(out_ref.shape[0]):
        out_ref[target] = total


def leave_kernel(in_ref, out_hbm, left):
    count = left.shape[0]
    part = in_ref.shape[1] // count
    copies = [
        pltpu.make_async_copy(in_ref.at[:, pl.ds(at * part, part)], out_hbm.at[:, pl.ds(at * part, part)], left.at[at])
        for at in range(count)]
    for copy in copies:
        copy.start()
    for copy in copies:
        copy.wait()


def call(kernel, out_shape, operands, scratch=(), spaces=(), limit=VMEM_LIMIT, out_space=pltpu.VMEM):
    spaces = tuple(spaces) + (pltpu.VMEM,) * (len(operands) - len(spaces))
    return pl.pallas_call(
        kernel,
        out_shape=jax.ShapeDtypeStruct(out_shape, BF16),
        in_specs=[pl.BlockSpec(memory_space=space) for space in spaces],
        out_specs=pl.BlockSpec(memory_space=out_space),
        scratch_shapes=list(scratch),
        compiler_params=pltpu.CompilerParams(vmem_limit_bytes=limit),
        cost_estimate=pl.CostEstimate(flops=1000000, bytes_accessed=2000000, transcendentals=0),
    )(*operands)


def landing(arrays):
    return [pltpu.VMEM(array.shape, array.dtype) for array in arrays], pltpu.SemaphoreType.DMA((len(arrays),))


def exchange(array, axis, groups=None):
    return lax.all_to_all(array, axis, split_axis=0, concat_axis=0, tiled=True, axis_index_groups=groups)


def local(increment, mask, members, weight, x_inverse, x_coupling, y_inverse, y_coupling):
    _, _, rows, columns = members.shape
    space, mem = lax.axis_size("space"), lax.axis_size("mem")
    x_blocks, y_blocks = x_inverse.shape[0], y_inverse.shape[0]
    close = 8
    apart = mem // close
    near_groups = [[z * close + i for i in range(close)] for z in range(apart)]
    far_groups = [[z * close + i for z in range(apart)] for i in range(close)]
    share = (HALF + FOLD, BLOCK)

    y_tables = prepare(y_inverse, y_coupling)
    x_tables = prepare(x_inverse, x_coupling)

    inputs = (increment, mask, members, weight)
    near, arrived = landing(inputs)
    sent = call(start_kernel, (space,) + share, inputs,
                near + [arrived], [pltpu.HBM] * 4, WIDE_LIMIT)
    got, x_tables, y_tables = lax.optimization_barrier((exchange(sent, "space"), x_tables, y_tables))
    sent = call(functools.partial(column_kernel, y_blocks), (space,) + share, (got,) + tuple(y_tables),
                [pltpu.VMEM((BLOCK + EXTRA, y_blocks * BLOCK), BF16)])
    got = exchange(sent, "space")
    own = (lax.axis_index("mem") % close).astype(jnp.int32)[None]
    packed = (rows // close, columns)
    inputs = (members, weight)
    near, arrived = landing(inputs)
    terms = call(functools.partial(row_kernel, x_blocks), (close,) + packed,
                 (got,) + inputs + tuple(x_tables),
                 near + [pltpu.VMEM((rows, columns), BF16), arrived],
                 [pltpu.VMEM, pltpu.HBM, pltpu.HBM])
    terms = exchange(terms, "mem", near_groups)
    part = call(sum_kernel, (1,) + packed, (terms,))
    for step in range(2):
        pairs = []
        for device in range(mem):
            z, odd = device // close, (device + step) % 2
            pairs.append((device, ((z ^ 1) if odd == 0 else ((z - 1) ^ 1) + 1) % apart * close + device % close))
        other = lax.ppermute(part, "mem", pairs)
        if step == 0:
            part = call(add_kernel, (1,) + packed, (part, other))
    result = call(functools.partial(final_kernel, float(mem - 1)), (close,) + packed, (own, part, other, mask),
                  spaces=[pltpu.SMEM])
    result = exchange(result, "mem", near_groups).reshape(1, rows, columns)
    return call(leave_kernel, (1, rows, columns), (result,), [pltpu.SemaphoreType.DMA((4,))], out_space=pltpu.HBM)


def solution(mesh):
    placed = (
        P(None, "space", None),
        P(None, "space", None),
        P("mem", None, "space", None),
        P("space", None),
        P(),
        P(),
        P(),
        P(),
    )
    return jax.shard_map(
        local, mesh=mesh, in_specs=placed, out_specs=P(None, "space", None), check_vma=False
    )
```
